32 devices in a mesh: groups: 2 (over x), gx: 4 (over y, core), gy: 4 (over z).
Axes of the slice: x: 2, y: 2, z: 4, core: 2. Of those that a mesh axis runs over, the one named last changes fastest.
Arguments:
- field_input: bfloat16 [64, 256, 1024], P(('groups', 'gx'), 'gy'), parts along dimension 0, may hold values from -8 to 8
- cotangent: bfloat16 [64, 256, 1024], P(('groups', 'gx'), 'gy'), parts along dimension 0, may hold values from -8 to 8
- spectral_weight: bfloat16 [256, 32768], P(('gx', 'gy')), may hold values from -0.75 to 0.75
- point_weight: bfloat16 [32, 32], replicated, may hold values from -1 to 1
- point_bias: float32 [32], replicated, may hold values from -3 to 3
Outputs:
- grad_field: bfloat16 [64, 256, 1024], P(('groups', 'gx'), 'gy'), parts along dimension 0
- grad_spectral: float32 [512, 32768], P(('groups', 'gx', 'gy')), parts along dimension 0
- grad_point: float32 [64, 32], P('groups'), parts along dimension 0
- grad_bias: float32 [64], P('groups'), parts along dimension 0
The draws below stay inside these ranges and needn't reach their ends.
There are 2 independent parts, one for each index of `groups`. The reference program is written for one: setup_inputs(seed, part) draws one part's arguments, and reference() takes and returns one part's arrays. A program takes and returns all parts, laid end to end along the dimension named above; an argument that names none is the same for every part. Nothing has to cross between parts.
All inputs are finite; a program needn't handle non-finite values.
Results may differ from the reference program's by a relative error of at most 0.0052.
Values sent between devices are 32-bit elements; how exact they have to be, the bound alone decides.
A program may use at most 64 MiB of HBM per device.

```python
import math
import jax
import jax.numpy as jnp
from jax import lax

C = 32
KX = 16
KY = 16
KZ = 16
NZ = 32
CX = 8
NX = 32
NY = 256


def series_draw(seed_key, series_count, mode_count, length):
    coeffs = jax.random.normal(seed_key, (series_count, mode_count, 2), jnp.float32)
    steps = jnp.arange(mode_count, dtype=jnp.int32)[:, None] * jnp.arange(length, dtype=jnp.int32)[None, :] % length
    angles = 2.0 * math.pi / length * steps.astype(jnp.float32)
    waves = coeffs[:, :, 0:1] * jnp.cos(angles)[None] + coeffs[:, :, 1:2] * jnp.sin(angles)[None]
    return jnp.sum(waves, axis=1) / math.sqrt(mode_count)


def smooth_field(seed_key):
    keys = jax.random.split(seed_key, 3)
    along_x = series_draw(keys[0], 4, KX // 2, NX)
    along_y = series_draw(keys[1], 4, KY // 2, NY)
    along_z = series_draw(keys[2], 4 * C, KZ, NZ).reshape(4, C, NZ).transpose(0, 2, 1).reshape(4, NZ * C)
    plane = along_x[:, :, None] * along_y[:, None, :]
    return jnp.einsum('jab,jm->abm', plane, along_z) / 2.0


def mixed_field(seed_key):
    keys = jax.random.split(seed_key, 2)
    smooth = smooth_field(keys[0])
    values = jax.random.normal(keys[1], (NX, NY, NZ * C), jnp.float32) + smooth
    return jnp.clip(values, -8.0, 8.0).astype(jnp.bfloat16)


def draw_field_input(key, part):
    return mixed_field(jax.random.fold_in(key, 11))


def draw_cotangent(key, part):
    return mixed_field(jax.random.fold_in(key, 23))


def block_scale(own_key, shape, cuts, least, high):
    factor_of = 1.0
    for dim, blocks in cuts:
        draws = jax.random.uniform(jax.random.fold_in(jax.random.fold_in(own_key, 6), dim), (blocks,), jnp.float32, least / len(cuts), high / len(cuts))
        factor_of = factor_of * jnp.repeat(jnp.exp(draws), shape[dim] // blocks).reshape((-1,) + (1,) * (len(shape) - 1 - dim))
    return factor_of


def centred(rng, dims, spread, bound, cuts=(), kind=jnp.bfloat16):
    array = spread * jax.random.normal(rng, dims, jnp.float32)
    if cuts:
        array = array * block_scale(rng, dims, cuts, -0.22, 0.18)
    return jnp.clip(array, -bound, bound).astype(kind)


def setup_inputs(seed: int = 0, part: int = 0) -> dict:
    seeds = jax.random.split(jax.random.key(seed), 6)
    part_keys = jax.random.split(jax.random.fold_in(seeds[5], part), 6)
    field_input = draw_field_input(jax.random.fold_in(jax.random.fold_in(seeds[5], part), 71), part)
    cotangent = draw_cotangent(jax.random.fold_in(jax.random.fold_in(seeds[5], part), 71), part)
    spectral_weight = centred(seeds[2], (KY * KZ, KX * 2 * C * C), (2 * C) ** -0.5, 0.75, ((0, 16),))
    point_weight = centred(seeds[3], (C, C), C ** -0.5, 1.0)
    point_bias = centred(seeds[4], (C,), 0.5, 3.0, (), jnp.float32)
    return {"field_input": field_input, "cotangent": cotangent, "spectral_weight": spectral_weight, "point_weight": point_weight, "point_bias": point_bias}


def mode_values(mode_count, length):
    position = jnp.arange(mode_count, dtype=jnp.int32)
    return jnp.where(position < mode_count // 2, position, length - mode_count + position).astype(jnp.int32)

def phase_angles(positions, wavenumbers, length):
    steps = positions[:, None] * wavenumbers[None, :] % length
    return 2.0 * math.pi / length * steps.astype(jnp.float32)

def complex_table(positions, wavenumbers, length, factor):
    angles = phase_angles(positions, wavenumbers, length)
    cosine = jnp.cos(angles) * factor
    sine = jnp.sin(angles) * factor
    return jnp.stack([jnp.stack([cosine, -sine], axis=-1), jnp.stack([sine, cosine], axis=-1)], axis=1)

def depth_table(depth_count, mode_count):
    angles = phase_angles(jnp.arange(depth_count, dtype=jnp.int32), jnp.arange(mode_count, dtype=jnp.int32), depth_count)
    return jnp.stack([jnp.cos(angles), -jnp.sin(angles)], axis=1).astype(jnp.bfloat16)

def doubled(table):
    factor = jnp.where(jnp.arange(table.shape[2]) == 0, 1.0, 2.0).astype(jnp.float32)
    return table.astype(jnp.float32) * factor[None, None, :]

def spectral_product(spectrum, weights):
    shaped = spectrum.reshape(spectrum.shape[0], KX, 2, C)
    real_in, imag_in = (shaped[:, :, 0], shaped[:, :, 1])
    real_w, imag_w = (weights[:, :, 0], weights[:, :, 1])
    hp = lax.Precision.HIGHEST
    real_out = jnp.einsum('rmi,rmio->rmo', real_in, real_w, precision=hp) - jnp.einsum('rmi,rmio->rmo', imag_in, imag_w, precision=hp)
    imag_out = jnp.einsum('rmi,rmio->rmo', real_in, imag_w, precision=hp) + jnp.einsum('rmi,rmio->rmo', imag_in, real_w, precision=hp)
    return jnp.stack([real_out, imag_out], axis=2).reshape(spectrum.shape)

def adjoint_product(spectrum, weights):
    shaped = spectrum.reshape(spectrum.shape[0], KX, 2, C)
    real_in, imag_in = (shaped[:, :, 0], shaped[:, :, 1])
    real_w, imag_w = (weights[:, :, 0], weights[:, :, 1])
    hp = lax.Precision.HIGHEST
    real_out = jnp.einsum('rmo,rmio->rmi', real_in, real_w, precision=hp) + jnp.einsum('rmo,rmio->rmi', imag_in, imag_w, precision=hp)
    imag_out = jnp.einsum('rmo,rmio->rmi', imag_in, real_w, precision=hp) - jnp.einsum('rmo,rmio->rmi', real_in, imag_w, precision=hp)
    return jnp.stack([real_out, imag_out], axis=2).reshape(spectrum.shape)

def weight_gradient(field_spec, adjoint_spec):
    field_shaped = field_spec.reshape(field_spec.shape[0], KX, 2, C)
    adjoint_shaped = adjoint_spec.reshape(adjoint_spec.shape[0], KX, 2, C)
    real_v, imag_v = (field_shaped[:, :, 0], field_shaped[:, :, 1])
    real_h, imag_h = (adjoint_shaped[:, :, 0], adjoint_shaped[:, :, 1])
    real_g = real_v[:, :, :, None] * real_h[:, :, None, :] + imag_v[:, :, :, None] * imag_h[:, :, None, :]
    imag_g = real_v[:, :, :, None] * imag_h[:, :, None, :] - imag_v[:, :, :, None] * real_h[:, :, None, :]
    return jnp.stack([real_g, imag_g], axis=2).reshape(field_spec.shape[0], KX * 2 * C * C)

def forward_block(values, z_table, y_table, x_block):
    block_rows = values.shape[0]
    hp = lax.Precision.HIGHEST
    shaped = values.reshape(block_rows, NY, NZ, C).astype(jnp.float32)
    zpart = jnp.einsum('xyzc,zpk->xypkc', shaped, z_table.astype(jnp.float32), precision=hp).reshape(block_rows, NY, 2, KZ * C)
    ypart = jnp.einsum('xyqm,yqjp->xjpm', zpart, y_table, precision=hp).reshape(block_rows, KY, 2, KZ, C)
    xpart = jnp.einsum('xjqkc,xqmp->jkmpc', ypart, x_block, precision=hp)
    return xpart.reshape(KY * KZ, KX * 2 * C)

def inverse_block(spectrum, z_float, y_table, x_block):
    block_rows = x_block.shape[0]
    hp = lax.Precision.HIGHEST
    shaped = spectrum.reshape(KY, KZ, KX, 2, C)
    xpart = jnp.einsum('jkmqc,xpmq->xjpkc', shaped, x_block, precision=hp).reshape(block_rows, KY, 2, KZ * C)
    ypart = jnp.einsum('xjqm,ypjq->xypm', xpart, y_table, precision=hp).reshape(block_rows, NY, 2, KZ, C)
    return jnp.einsum('xypkc,zpk->xyzc', ypart, z_float, precision=hp).reshape(block_rows, NY, NZ * C)

def channel_mix(values, weight):
    rows = values.reshape(-1, C)
    return jnp.dot(rows, weight, preferred_element_type=jnp.float32).reshape(values.shape)

def reference(field_input, cotangent, spectral_weight, point_weight, point_bias):
    cell_scale = 1.0 / math.sqrt(NX * NY * NZ)
    block_count = NX // CX
    z_plain = depth_table(NZ, KZ)
    z_double = doubled(z_plain).astype(jnp.bfloat16)
    y_table = complex_table(jnp.arange(NY, dtype=jnp.int32), mode_values(KY, NY), NY, 1.0)
    x_table = complex_table(jnp.arange(NX, dtype=jnp.int32), mode_values(KX, NX), NX, cell_scale)
    x_blocks = x_table.reshape(block_count, CX, 2, KX, 2)
    field_blocks = field_input.reshape(block_count, CX, NY, NZ * C)
    cot_blocks = cotangent.reshape(block_count, CX, NY, NZ * C)
    empty = jnp.zeros((KY * KZ, KX * 2 * C), jnp.float32)

    def forward_step(running, items):
        values, x_block = items
        return (running + forward_block(values, z_plain, y_table, x_block), None)
    field_spec, _ = lax.scan(forward_step, empty, (field_blocks, x_blocks))
    weights = spectral_weight.astype(jnp.float32).reshape(KY * KZ, KX, 2, C, C)
    mode_output = spectral_product(field_spec, weights)
    bias_row = jnp.tile(point_bias, NZ)
    z_double_float = doubled(z_plain)

    def backward_step(carry, items):
        adjoint_spec, point_sum, bias_sum = carry
        values, cot_block, x_block = items
        spectral_out = inverse_block(mode_output, z_double_float, y_table, x_block)
        preact = spectral_out + channel_mix(values, point_weight) + bias_row
        _, pullback = jax.vjp(jax.nn.gelu, preact)
        adjoint = pullback(cot_block.astype(jnp.float32))[0].astype(jnp.bfloat16)
        adjoint_spec = adjoint_spec + forward_block(adjoint, z_double, y_table, x_block)
        flat_values = values.reshape(-1, C)
        flat_adjoint = adjoint.reshape(-1, C)
        point_sum = point_sum + jnp.dot(flat_values.T, flat_adjoint, preferred_element_type=jnp.float32)
        bias_sum = bias_sum + lax.optimization_barrier(jnp.sum(flat_adjoint.astype(jnp.float32), axis=0))
        return ((adjoint_spec, point_sum, bias_sum), adjoint)
    start = (empty, jnp.zeros((C, C), jnp.float32), jnp.zeros((C,), jnp.float32))
    (adjoint_spec, point_sum, bias_sum), adjoint_all = lax.scan(backward_step, start, (field_blocks, cot_blocks, x_blocks))
    grad_spectral = weight_gradient(field_spec, adjoint_spec) * cell_scale
    mode_adjoint = adjoint_product(adjoint_spec, weights)
    z_plain_float = z_plain.astype(jnp.float32)

    def final_block(items):
        adjoint, x_block = items
        back_field = inverse_block(mode_adjoint, z_plain_float, y_table, x_block)
        return (channel_mix(adjoint, point_weight.T) + back_field).astype(jnp.bfloat16)
    grad_field = lax.map(final_block, (adjoint_all, x_blocks)).reshape(NX, NY, NZ * C)
    return (grad_field, grad_spectral, point_sum * cell_scale, bias_sum * cell_scale)
```

```python
import functools
import math

import jax
import jax.numpy as jnp
import numpy as np
from jax import lax
from jax.experimental import pallas as pl
from jax.experimental.pallas import tpu as pltpu
from jax.sharding import PartitionSpec as P

C = 32
KX = 16
KY = 16
KZ = 16
NZ = 32
PM = 2 * KX
F32 = jnp.float32
BF16 = jnp.bfloat16
HIGH = lax.Precision.HIGHEST
MESH = pl.DeviceIdType.MESH


def modes(count, length):
    position = np.arange(count)
    return np.where(position < count // 2, position, length - count + position)


def angles(positions, wavenumbers, length):
    steps = positions[:, None] * wavenumbers[None, :] % length
    return 2.0 * math.pi / length * steps.astype(np.float64)


def tables(ngx, ngy, rows_x, rows_y, kk):
    full_x, full_y = ngx * rows_x, ngy * rows_y
    blocks = KZ // kk
    scale = 1.0 / math.sqrt(full_x * full_y * NZ)
    tz = angles(np.arange(NZ), np.arange(KZ), NZ)
    cz, sz = np.cos(tz), np.sin(tz)
    core = np.stack([np.stack([cz, -sz], 1), np.stack([sz, cz], 1)], 0)
    core = core.reshape(2 * NZ, 2, blocks, kk).transpose(0, 2, 1, 3).reshape(2 * NZ, 2 * KZ)
    to_modes = np.kron(core.astype(np.float32), np.eye(C, dtype=np.float32))
    ty = angles(np.arange(full_y), modes(KY, full_y), full_y).reshape(ngy, rows_y, KY)
    ytab = np.stack([np.cos(ty), -np.sin(ty)], 1).transpose(0, 1, 3, 2)
    ybd = np.einsum("gqjy,xw->gqjxwy", ytab, np.eye(rows_x))
    ybd = ybd.reshape(ngy, 2 * KY * rows_x, rows_x * rows_y)
    tx = angles(np.arange(full_x), modes(KX, full_x), full_x).T
    cx, sx = np.cos(tx) * scale, np.sin(tx) * scale
    xf = np.concatenate(
        [np.concatenate([cx, sx], 1), np.concatenate([-sx, cx], 1)], 0
    )
    n = PM * kk
    perm = np.zeros((n, n))
    r = np.arange(n)
    perm[r, (r % kk) * PM + r // kk] = 1.0
    eye = np.eye(C)
    over_out = np.repeat(eye, C, axis=1)
    over_in = np.tile(eye, (1, C))
    bf = lambda a: jnp.asarray(np.ascontiguousarray(a).astype(jnp.bfloat16))
    f32 = lambda a: jnp.asarray(np.ascontiguousarray(a).astype(np.float32))
    return dict(
        ybd=bf(ybd),
        gz=bf(to_modes),
        xf=f32(xf),
        perm=bf(perm),
        ei=bf(np.concatenate([over_out, over_out], 0)),
        ro=bf(np.tile(eye, (4, 1))),
        ybt=bf(ybd.transpose(0, 2, 1)),
        xs=f32(xf.T),
        hz=bf(to_modes.T),
        permt=bf(perm.T),
        eo=bf(np.concatenate([over_in, over_in], 0)),
        ri=bf(over_out.T),
    )


TABLES = ["ybd", "gz", "xf", "perm", "ei", "ro", "ybt", "xs", "hz", "permt", "eo", "ri"]
BY_GY = ("ybd", "ybt")


def dot(a, b):
    return jnp.dot(a, b, preferred_element_type=F32)


def dot32(a, b):
    return jnp.dot(a, b, preferred_element_type=F32, precision=HIGH)


def split(a):
    high = a.astype(BF16)
    return high, (a - high.astype(F32)).astype(BF16)


def kernel(ngx, ngy, rx, ry, kk, names, *refs):
    it = iter(refs)
    hbm = {name: next(it) for name in names}
    wp_ref, bias_ref = next(it), next(it)
    gf_out, gs_out, gp_out, gb_out = (next(it) for _ in range(4))
    vm = {name: next(it) for name in names}
    (ybuf, zout, recv1, send2, recv2, zs, recvs, fs, fin, gq, vexp, hexp, red, prod,
     adj, gs, acc, accb, kw, pbuf, precv, pbuf2, precv2) = (next(it) for _ in range(23))
    (in_sem, gs_sem, s1_send, s1_recv, s2_send, s2_recv, g_send, g_recv, f_send, f_recv,
     p_send, p_recv) = (next(it) for _ in range(12))

    gx, gy = lax.axis_index("gx"), lax.axis_index("gy")
    nx = ngx * rx
    half = kk * C
    width = 2 * half
    blocks = KZ // kk
    n = KX * kk
    scale = 1.0 / math.sqrt(nx * ngy * ry * NZ)

    loads = {}
    for i, name in enumerate(names):
        src = hbm[name].at[gy] if name in BY_GY else hbm[name]
        loads[name] = pltpu.make_async_copy(src, vm[name], in_sem.at[i])
        loads[name].start()

    barrier = pltpu.get_barrier_semaphore()
    for e in range(1, ngx):
        pl.semaphore_signal(barrier, inc=1, device_id={"gx": lax.rem(gx + e, ngx)}, device_id_type=MESH)
    for d in range(1, ngy):
        pl.semaphore_signal(barrier, inc=1, device_id={"gy": lax.rem(gy + d, ngy)}, device_id_type=MESH)

    def slab(ref, owner):
        rows = pl.ds(pl.multiple_of(owner // blocks * rx, rx), rx)
        if blocks == 1:
            return ref.at[rows]
        return ref.at[rows, pl.ds(pl.multiple_of(owner % blocks * width, width), width)]

    def lanes(b):
        return pl.ds(pl.multiple_of(b * 256, 256), 256)

    pending = []

    def forward(t, u):
        @pl.loop(0, 4)
        def _(b):
            value = dot(vm["ybd"][...], u[:, lanes(b)]).astype(BF16)
            ybuf[:, lanes(b)] = value
        if t == 0:
            loads["gz"].wait()
        rows = KY * rx

        @pl.loop(0, 4)
        def _(b):
            zout[t, :, lanes(b)] = dot(ybuf[:rows], vm["gz"][: NZ * C, lanes(b)]) + dot(
                ybuf[rows:], vm["gz"][NZ * C :, lanes(b)]
            )
        if t == 0:
            pl.semaphore_wait(barrier, ngx + ngy - 2)
        mine = pl.ds(pl.multiple_of(gx * rx, rx), rx)
        order = list(range(1, ngy)) + [0]
        for d in order:
            g = lax.rem(gy + d, ngy)
            for e in range(1, ngx):
                to = lax.rem(gx + e, ngx)
                copy = pltpu.make_async_remote_copy(
                    src_ref=slab(zout.at[t], to * ngy + g),
                    dst_ref=recv1.at[t, g, mine],
                    send_sem=s1_send.at[t, d, e - 1],
                    recv_sem=s1_recv.at[t, g],
                    device_id={"gx": to},
                    device_id_type=MESH,
                )
                copy.start()
                pending.append(copy)
            recv1[t, g, mine] = slab(zout.at[t], gx * ngy + g)[...]

    def gather_modes(t):
        order = list(range(1, ngy)) + [0]
        for d in order:
            g = lax.rem(gy + d, ngy)
            got = recv1.at[t, g, pl.ds(0, (ngx - 1) * rx)]
            pltpu.make_async_copy(got, got, s1_recv.at[t, g]).wait()
            value = dot32(vm["xf"][:, :nx], recv1[t, g, :, :half]) + dot32(
                vm["xf"][:, nx:], recv1[t, g, :, half:]
            )
            if d == 0:
                recv2[t, gy] = value
            else:
                send2[t, d] = value
                copy = pltpu.make_async_remote_copy(
                    src_ref=send2.at[t, d],
                    dst_ref=recv2.at[t, gy],
                    send_sem=s2_send.at[t, d],
                    recv_sem=s2_recv.at[t],
                    device_id={"gy": g},
                    device_id_type=MESH,
                )
                copy.start()
                pending.append(copy)
        got = recv2.at[t, pl.ds(0, ngy - 1)]
        pltpu.make_async_copy(got, got, s2_recv.at[t]).wait()
        total = recv2[t, 0]
        for g in range(1, ngy):
            total = total + recv2[t, g]
        return total

    def scatter_modes(t, value):
        zs[t] = value
        for d in range(1, ngy):
            copy = pltpu.make_async_remote_copy(
                src_ref=zs.at[t],
                dst_ref=recvs.at[t, gy],
                send_sem=g_send.at[t, d],
                recv_sem=g_recv.at[t, gy],
                device_id={"gy": lax.rem(gy + d, ngy)},
                device_id_type=MESH,
            )
            copy.start()
            pending.append(copy)
        mine = pl.ds(pl.multiple_of(gx * rx, rx), rx)
        for d in range(ngy):
            g = lax.rem(gy + d, ngy)
            if d == 0:
                block = value
            else:
                got = recvs.at[t, g]
                pltpu.make_async_copy(got, got, g_recv.at[t, g]).wait()
                block = recvs[t, g]
            fs[t, g, :, :half] = dot32(vm["xs"][:nx], block)
            fs[t, g, :, half:] = dot32(vm["xs"][nx:], block)
            owner = gx * ngy + g
            for e in range(1, ngx):
                to = lax.rem(gx + e, ngx)
                copy = pltpu.make_async_remote_copy(
                    src_ref=fs.at[t, g, pl.ds(pl.multiple_of(to * rx, rx), rx)],
                    dst_ref=slab(fin.at[t], owner),
                    send_sem=f_send.at[t, d, e - 1],
                    recv_sem=f_recv.at[t],
                    device_id={"gx": to},
                    device_id_type=MESH,
                )
                copy.start()
                pending.append(copy)
            slab(fin.at[t], owner)[...] = fs[t, g, mine]

    def backward(t):
        got = fin.at[t, pl.ds(0, KY * rx // ngx * (ngx - 1))]
        pltpu.make_async_copy(got, got, f_recv.at[t]).wait()
        rows = KY * rx
        ybuf[:rows] = fin[t].astype(BF16)

        @pl.loop(0, 4)
        def _(b):
            gq[:rows, lanes(b)] = dot(ybuf[:rows], vm["hz"][:, lanes(b)]).astype(BF16)

        @pl.loop(0, 4)
        def _(b):
            gq[rows:, lanes(b)] = dot(ybuf[:rows], vm["hz"][:, lanes(b + 4)]).astype(BF16)

    def to_rows(value):
        stack = jnp.concatenate([value[:, k * C : (k + 1) * C] for k in range(kk)], axis=0)
        high = stack.astype(BF16).astype(F32)
        both = jnp.concatenate([high, stack - high], axis=1).astype(BF16)
        return dot(vm["perm"][...], both).astype(BF16)

    def from_rows(value):
        high = value.astype(BF16).astype(F32)
        both = jnp.concatenate([high, value - high], axis=1).astype(BF16)
        moved = dot(vm["permt"][...], both)
        moved = moved[:, :C] + moved[:, C:]
        return jnp.concatenate([moved[k * PM : (k + 1) * PM] for k in range(kk)], axis=1)

    lane = lax.broadcasted_iota(jnp.int32, (PM, half), 1)
    first_k = (gx * ngy + gy) % blocks * kk
    doubling = jnp.where(lane // C + first_k == 0, 1.0, 2.0).astype(F32)

    row = lax.broadcasted_iota(jnp.int32, (256, C), 0) % C
    col = lax.broadcasted_iota(jnp.int32, (256, C), 1)
    sel = (row == col).astype(F32).astype(BF16)
    tall = dot(sel, wp_ref[...]).astype(BF16)
    wide = lax.dot_general(tall, sel, (((1,), (1,)), ((), ())), preferred_element_type=F32)
    br = lax.broadcasted_iota(jnp.int32, (256, 256), 0) // C
    bc = lax.broadcasted_iota(jnp.int32, (256, 256), 1) // C
    kw[...] = jnp.where(br == bc, wide, 0.0).astype(BF16)
    bias = jnp.concatenate([bias_ref[...]] * 8, axis=1)

    loads["field"].wait()
    loads["ybd"].wait()
    forward(0, vm["field"])
    for name in names:
        if name not in ("field", "ybd", "gz"):
            loads[name].wait()
    spec = gather_modes(0)

    vexp[...] = dot(to_rows(spec), vm["ei"][...])
    for m in range(KX):
        a, b = slice(m * kk, (m + 1) * kk), slice(n + m * kk, n + (m + 1) * kk)
        vr, vi = vexp[a], vexp[b]
        wr = vm["weight"][:, m * 2048 : m * 2048 + 1024].astype(F32)
        wi = vm["weight"][:, m * 2048 + 1024 : m * 2048 + 2048].astype(F32)
        pr = vr * wr - vi * wi
        pi = vr * wi + vi * wr
        red[a] = sum(pr[:, s * 128 : (s + 1) * 128] for s in range(8))
        red[b] = sum(pi[:, s * 128 : (s + 1) * 128] for s in range(8))
    high, low = split(red[...])
    out = dot(high, vm["ro"][...]) + dot(low, vm["ro"][...])
    scatter_modes(0, from_rows(out) * doubling)
    backward(0)

    @pl.loop(0, 4)
    def _(b):
        mixed = dot(vm["field"][:, lanes(b)], kw[...])
        v = dot(vm["ybt"][...], gq[:, lanes(b)]) + mixed + bias
        root = math.sqrt(2.0 / math.pi)
        square = v * v
        th = jnp.tanh(root * v * (1.0 + 0.044715 * square))
        slope = 0.5 * (1.0 + th) + 0.5 * v * (1.0 - th * th) * (
            root * (1.0 + 3 * 0.044715 * square)
        )
        adj[:, lanes(b)] = (vm["cot"][:, lanes(b)].astype(F32) * slope).astype(BF16)

    forward(1, adj)

    acc[...] = jnp.zeros_like(acc)
    accb[...] = jnp.zeros_like(accb)
    ones = jnp.ones((16, rx * ry), BF16)

    @pl.loop(0, 4)
    def _(b):
        block = adj[:, lanes(b)]
        acc[...] += lax.dot_general(
            vm["field"][:, lanes(b)], block, (((0,), (0,)), ((), ())), preferred_element_type=F32
        )
        accb[...] += dot(ones, block)

    pbuf[...] = jnp.zeros_like(pbuf)
    pbuf[:C, :C] = sum(acc[i * C : (i + 1) * C, i * C : (i + 1) * C] for i in range(8)) * scale
    pbuf[C:, :C] = sum(accb[:8, i * C : (i + 1) * C] for i in range(8)) * scale
    for e in range(1, ngx):
        copy = pltpu.make_async_remote_copy(
            src_ref=pbuf,
            dst_ref=precv.at[gx],
            send_sem=p_send.at[e],
            recv_sem=p_recv.at[0],
            device_id={"gx": lax.rem(gx + e, ngx)},
            device_id_type=MESH,
        )
        copy.start()
        pending.append(copy)
    precv[gx] = pbuf[...]

    spec = gather_modes(1) * doubling
    hexp[...] = dot(to_rows(spec), vm["eo"][...])
    for m in range(KX):
        a, b = slice(m * kk, (m + 1) * kk), slice(n + m * kk, n + (m + 1) * kk)
        hr, hi = hexp[a], hexp[b]
        wr = vm["weight"][:, m * 2048 : m * 2048 + 1024].astype(F32)
        wi = vm["weight"][:, m * 2048 + 1024 : m * 2048 + 2048].astype(F32)
        prod[a] = hr * wr + hi * wi
        prod[b] = hi * wr - hr * wi
    high, low = split(prod[...])
    out = dot(high, vm["ri"][...]) + dot(low, vm["ri"][...])
    scatter_modes(1, from_rows(out))

    got = precv.at[pl.ds(0, ngx - 1)]
    pltpu.make_async_copy(got, got, p_recv.at[0]).wait()
    pbuf2[...] = sum(precv[i] for i in range(ngx))
    for d in range(1, ngy):
        copy = pltpu.make_async_remote_copy(
            src_ref=pbuf2,
            dst_ref=precv2.at[gy],
            send_sem=p_send.at[ngx + d],
            recv_sem=p_recv.at[1],
            device_id={"gy": lax.rem(gy + d, ngy)},
            device_id_type=MESH,
        )
        copy.start()
        pending.append(copy)
    precv2[gy] = pbuf2[...]

    for m in range(KX):
        a, b = slice(m * kk, (m + 1) * kk), slice(n + m * kk, n + (m + 1) * kk)
        vr, vi, hr, hi = vexp[a], vexp[b], hexp[a] * scale, hexp[b] * scale
        gs[:, m * 2048 : m * 2048 + 1024] = vr * hr + vi * hi
        gs[:, m * 2048 + 1024 : m * 2048 + 2048] = vr * hi - vi * hr
    gs_copy = pltpu.make_async_copy(gs, gs_out, gs_sem)
    gs_copy.start()

    backward(1)

    @pl.loop(0, 4)
    def _(b):
        back = lax.dot_general(
            adj[:, lanes(b)], kw[...], (((1,), (1,)), ((), ())), preferred_element_type=F32
        )
        gf_out[:, lanes(b)] = (dot(vm["ybt"][...], gq[:, lanes(b)]) + back).astype(BF16)

    got = precv2.at[pl.ds(0, ngy - 1)]
    pltpu.make_async_copy(got, got, p_recv.at[1]).wait()
    total = sum(precv2[i] for i in range(ngy))
    gp_out[...] = total[:C, :C]
    gb_out[...] = total[C : C + 1, :C]
    gs_copy.wait()
    for copy in pending:
        copy.wait_send()


def on_device(ngx, ngy, field_input, cotangent, spectral_weight, point_weight, point_bias):
    rx, ry, depth = field_input.shape
    kk = spectral_weight.shape[0]
    cells = rx * ry
    nx = rx * ngx
    half, width = kk * C, 2 * kk * C
    arrays = dict(field=field_input.reshape(cells, depth))
    consts = tables(ngx, ngy, rx, ry, kk)
    arrays["ybd"] = consts["ybd"]
    arrays["gz"] = consts["gz"]
    arrays["xf"] = consts["xf"]
    arrays["weight"] = spectral_weight
    for name in TABLES:
        arrays[name] = consts[name]
    arrays["cot"] = cotangent.reshape(cells, depth)
    names = tuple(arrays)
    local = [
        pltpu.VMEM(a.shape[1:] if k in BY_GY else a.shape, a.dtype) for k, a in arrays.items()
    ]
    rows = KY * rx
    n2 = PM * kk
    vmem = pl.BlockSpec(memory_space=pltpu.VMEM)
    hbm = pl.BlockSpec(memory_space=pl.ANY)
    dma = pltpu.SemaphoreType.DMA
    grad_field, grad_spectral, grad_point, grad_bias = pl.pallas_call(
        functools.partial(kernel, ngx, ngy, rx, ry, kk, names),
        out_shape=(
            jax.ShapeDtypeStruct((cells, depth), BF16),
            jax.ShapeDtypeStruct(spectral_weight.shape, F32),
            jax.ShapeDtypeStruct((C, C), F32),
            jax.ShapeDtypeStruct((1, C), F32),
        ),
        in_specs=[hbm] * len(names) + [vmem, vmem],
        out_specs=(vmem, hbm, vmem, vmem),
        scratch_shapes=local
        + [
            pltpu.VMEM((2 * rows, depth), BF16),
            pltpu.VMEM((2, rows, depth), F32),
            pltpu.VMEM((2, ngy, nx, width), F32),
            pltpu.VMEM((2, ngy, PM, half), F32),
            pltpu.VMEM((2, ngy, PM, half), F32),
            pltpu.VMEM((2, PM, half), F32),
            pltpu.VMEM((2, ngy, PM, half), F32),
            pltpu.VMEM((2, ngy, nx, width), F32),
            pltpu.VMEM((2, rows, depth), F32),
            pltpu.VMEM((2 * rows, depth), BF16),
            pltpu.VMEM((n2, C * C), F32),
            pltpu.VMEM((n2, C * C), F32),
            pltpu.VMEM((n2, 128), F32),
            pltpu.VMEM((n2, C * C), F32),
            pltpu.VMEM((cells, depth), BF16),
            pltpu.VMEM(spectral_weight.shape, F32),
            pltpu.VMEM((256, 256), F32),
            pltpu.VMEM((16, 256), F32),
            pltpu.VMEM((256, 256), BF16),
            pltpu.VMEM((C + 8, 128), F32),
            pltpu.VMEM((ngx, C + 8, 128), F32),
            pltpu.VMEM((C + 8, 128), F32),
            pltpu.VMEM((ngy, C + 8, 128), F32),
            dma((len(names),)),
            dma,
            dma((2, ngy, ngx - 1)),
            dma((2, ngy)),
            dma((2, ngy)),
            dma((2,)),
            dma((2, ngy)),
            dma((2, ngy)),
            dma((2, ngy, ngx - 1)),
            dma((2,)),
            dma((ngx + ngy,)),
            dma((2,)),
        ],
        compiler_params=pltpu.CompilerParams(
            collective_id=0, has_side_effects=True, vmem_limit_bytes=52 * 1024 * 1024
        ),
    )(*arrays.values(), point_weight, point_bias.reshape(1, C))
    return (
        grad_field.reshape(rx, ry, depth),
        grad_spectral,
        grad_point,
        grad_bias.reshape(C),
    )


def solution(mesh):
    return jax.shard_map(
        functools.partial(on_device, mesh.shape["gx"], mesh.shape["gy"]),
        mesh=mesh,
        in_specs=(
            P(("groups", "gx"), "gy", None),
            P(("groups", "gx"), "gy", None),
            P(("gx", "gy"), None),
            P(),
            P(),
        ),
        out_specs=(
            P(("groups", "gx"), "gy", None),
            P(("groups", "gx", "gy"), None),
            P("groups", None),
            P("groups"),
        ),
        check_vma=False,
    )
```

```python
import functools
import math

import jax
import jax.numpy as jnp
import numpy as np
from jax import lax
from jax.experimental import pallas as pl
from jax.experimental.pallas import tpu as pltpu
from jax.sharding import PartitionSpec as P

C = 32
KX = 16
KY = 16
KZ = 16
NZ = 32
PM = 2 * KX
F32 = jnp.float32
BF16 = jnp.bfloat16
MESH = pl.DeviceIdType.MESH


def modes(count, length):
    position = np.arange(count)
    return np.where(position < count // 2, position, length - count + position)


def angles(positions, wavenumbers, length):
    steps = positions[:, None] * wavenumbers[None, :] % length
    return 2.0 * math.pi / length * steps.astype(np.float64)


def tables(ngx, ngy, rows_x, rows_y, kk):
    full_x, full_y = ngx * rows_x, ngy * rows_y
    scale = 1.0 / math.sqrt(full_x * full_y * NZ)
    tz = angles(np.arange(NZ), np.arange(KZ), NZ)
    eye = np.eye(C, dtype=np.float32)
    to_modes = np.concatenate(
        [np.kron(f(tz).astype(np.float32), eye) for f in (np.cos, np.sin)], 1
    )
    from_modes = np.concatenate(
        [np.kron(f(tz).astype(np.float32).T, eye) for f in (np.cos, np.sin)], 1
    )
    ty = angles(np.arange(full_y), modes(KY, full_y), full_y).reshape(ngy, rows_y, KY)
    ytab = np.stack([np.cos(ty), -np.sin(ty)], 1).transpose(0, 1, 3, 2)
    ybd = np.einsum("gqjy,xw->gqjxwy", ytab, np.eye(rows_x))
    ybd = ybd.reshape(ngy, 2 * KY * rows_x, rows_x * rows_y)
    tx = angles(np.arange(full_x), modes(KX, full_x), full_x).T
    cx, sx = np.cos(tx) * scale, np.sin(tx) * scale
    xf = np.concatenate(
        [np.concatenate([cx, sx], 1), np.concatenate([-sx, cx], 1)], 0
    )
    bf = lambda a: np.ascontiguousarray(a).astype(jnp.bfloat16)

    def three(a):
        high = bf(a)
        low = bf(a - high.astype(np.float64))
        return jnp.asarray(np.concatenate([high, high, low], 1))

    return dict(
        ybd=jnp.asarray(bf(ybd)),
        gz=jnp.asarray(bf(to_modes)),
        xf=three(xf),
        ybt=jnp.asarray(bf(ybd.transpose(0, 2, 1))),
        xs=three(xf.T),
        hz=jnp.asarray(bf(from_modes)),
    )


TABLES = ["ybd", "gz", "xf", "ybt", "xs", "hz"]
BY_GY = ("ybd", "ybt")


def dot(a, b):
    return jnp.dot(a, b, preferred_element_type=F32)


def dot3(table, b):
    high, low = split(b)
    return dot(table, jnp.concatenate([high, low, high], axis=0))


def split(a):
    high = a.astype(BF16)
    return high, (a - high.astype(F32)).astype(BF16)


def kernel(ngx, ngy, rx, ry, kk, names, *refs):
    it = iter(refs)
    hbm = {name: next(it) for name in names}
    gf_out, gs_out, gp_out, gb_out = (next(it) for _ in range(4))
    vm = {name: next(it) for name in names}
    (ybuf, zout, recv1, send2, recv2, zs, recvs, fs, fin, gq, vexp, hexp, red, prod,
     adj, gs, acc, accb, kw, pbuf, precv, pbuf2, precv2, f2, pre, gf, perm, permt, ei, eo,
     ro, ri) = (next(it) for _ in range(32))
    (in_sem, gs_sem, gf_sem, s1_send, s1_recv, s2_send, s2_recv, g_send, g_recv, f_send, f_recv,
     p_send, p_recv) = (next(it) for _ in range(13))

    gx, gy = lax.axis_index("gx"), lax.axis_index("gy")
    nx = ngx * rx
    half = kk * C
    width = 2 * half
    blocks = KZ // kk
    n = KX * kk
    scale = 1.0 / math.sqrt(nx * ngy * ry * NZ)

    loads = {}
    for i, name in enumerate(names):
        src = hbm[name].at[gy] if name in BY_GY else hbm[name]
        loads[name] = pltpu.make_async_copy(src, vm[name], in_sem.at[i])
        loads[name].start()

    barrier = pltpu.get_barrier_semaphore()
    for e in range(1, ngx):
        pl.semaphore_signal(barrier, inc=1, device_id={"gx": lax.rem(gx + e, ngx)}, device_id_type=MESH)
    for d in range(1, ngy):
        pl.semaphore_signal(barrier, inc=1, device_id={"gy": lax.rem(gy + d, ngy)}, device_id_type=MESH)

    def slab(ref, owner):
        rows = pl.ds(pl.multiple_of(owner // blocks * rx, rx), rx)
        if blocks == 1:
            return ref.at[rows]
        return ref.at[rows, pl.ds(pl.multiple_of(owner % blocks * width, width), width)]

    def lanes(b):
        return pl.ds(pl.multiple_of(b * 256, 256), 256)

    chips = ngx // 2
    chip, core = gx // 2, gx % 2
    steps = [(c, k) for c in range(1, chips) for k in range(2)] + [(0, 1)]
    peers = [lax.rem(chip + c, chips) * 2 + lax.rem(core + k, 2) for c, k in steps]
    way = 1 - 2 * (gy // (ngy // 2))

    def along(d):
        return lax.rem(gy + way * d + ngy, ngy)

    far_first = list(range(ngy - 1, -1, -1))
    pending = []

    rows = KY * rx

    def forward(t, u):
        for b in range(4):
            at = slice(b * 256, b * 256 + 256)
            ybuf[:, at] = dot(vm["ybd"][...], u[:, at]).astype(BF16)
        if t == 0:
            loads["gz"].wait()
        for b in range(2):
            cos = dot(ybuf[...], vm["gz"][:, b * 256 : b * 256 + 256])
            sin = dot(ybuf[...], vm["gz"][:, KZ * C + b * 256 : KZ * C + b * 256 + 256])
            real = cos[:rows] + sin[rows:]
            imag = cos[rows:] - sin[:rows]
            part = min(half, 256)
            for i in range(256 // part):
                lane0 = b * 256 + i * part
                at = lane0 // half * width + lane0 % half
                zout[t, :, at : at + part] = real[:, i * part : (i + 1) * part]
                zout[t, :, at + half : at + half + part] = imag[:, i * part : (i + 1) * part]
        if t == 0:
            pl.semaphore_wait(barrier, ngx + ngy - 2)
        mine = pl.ds(pl.multiple_of(gx * rx, rx), rx)
        for d in far_first:
            g = along(d)
            for e, to in enumerate(peers):
                copy = pltpu.make_async_remote_copy(
                    src_ref=slab(zout.at[t], to * ngy + g),
                    dst_ref=recv1.at[t, g, mine],
                    send_sem=s1_send.at[t, d, e],
                    recv_sem=s1_recv.at[t, g],
                    device_id={"gx": to},
                    device_id_type=MESH,
                )
                copy.start()
                pending.append(copy)
            recv1[t, g, mine] = slab(zout.at[t], gx * ngy + g)[...]

    def gather_modes(t):
        for d in far_first:
            g = along(d)
            got = recv1.at[t, g, pl.ds(0, (ngx - 1) * rx)]
            pltpu.make_async_copy(got, got, s1_recv.at[t, g]).wait()
            both = jnp.concatenate([recv1[t, g, :, :half], recv1[t, g, :, half:]], axis=0)
            value = dot3(vm["xf"][...], both)
            if d == 0:
                recv2[t, gy] = value
            else:
                send2[t, d] = value
                copy = pltpu.make_async_remote_copy(
                    src_ref=send2.at[t, d],
                    dst_ref=recv2.at[t, gy],
                    send_sem=s2_send.at[t, d],
                    recv_sem=s2_recv.at[t],
                    device_id={"gy": g},
                    device_id_type=MESH,
                )
                copy.start()
                pending.append(copy)
        got = recv2.at[t, pl.ds(0, ngy - 1)]
        pltpu.make_async_copy(got, got, s2_recv.at[t]).wait()
        total = recv2[t, 0]
        for g in range(1, ngy):
            total = total + recv2[t, g]
        return total

    def scatter_modes(t, value):
        zs[t] = value
        for d in range(1, ngy):
            copy = pltpu.make_async_remote_copy(
                src_ref=zs.at[t],
                dst_ref=recvs.at[t, gy],
                send_sem=g_send.at[t, d],
                recv_sem=g_recv.at[t, gy],
                device_id={"gy": along(d)},
                device_id_type=MESH,
            )
            copy.start()
            pending.append(copy)
        mine = pl.ds(pl.multiple_of(gx * rx, rx), rx)
        for d in range(ngy):
            g = along(d)
            if d == 0:
                block = value
            else:
                got = recvs.at[t, g]
                pltpu.make_async_copy(got, got, g_recv.at[t, g]).wait()
                block = recvs[t, g]
            both = dot3(vm["xs"][...], block)
            fs[t, g, :, :half] = both[:nx]
            fs[t, g, :, half:] = both[nx:]
            owner = gx * ngy + g
            for e, to in enumerate(peers):
                copy = pltpu.make_async_remote_copy(
                    src_ref=fs.at[t, g, pl.ds(pl.multiple_of(to * rx, rx), rx)],
                    dst_ref=slab(fin.at[t], owner),
                    send_sem=f_send.at[t, d, e],
                    recv_sem=f_recv.at[t],
                    device_id={"gx": to},
                    device_id_type=MESH,
                )
                copy.start()
                pending.append(copy)
            slab(fin.at[t], owner)[...] = fs[t, g, mine]

    def backward(t):
        got = fin.at[t, pl.ds(0, KY * rx // ngx * (ngx - 1))]
        pltpu.make_async_copy(got, got, f_recv.at[t]).wait()
        for kb in range(blocks):
            at, to = kb * width, slice(kb * half, (kb + 1) * half)
            f2[:rows, to] = fin[t, :, at : at + half].astype(BF16)
            f2[rows:, to] = fin[t, :, at + half : at + width].astype(BF16)
        for b in range(4):
            at = slice(b * 256, b * 256 + 256)
            cos = dot(f2[...], vm["hz"][:, at])
            sin = dot(f2[...], vm["hz"][:, NZ * C + b * 256 : NZ * C + b * 256 + 256])
            gq[:rows, at] = (cos[:rows] - sin[rows:]).astype(BF16)
            gq[rows:, at] = (sin[:rows] + cos[rows:]).astype(BF16)

    def to_rows(value):
        stack = jnp.concatenate([value[:, k * C : (k + 1) * C] for k in range(kk)], axis=0)
        high = stack.astype(BF16).astype(F32)
        both = jnp.concatenate([high, stack - high], axis=1).astype(BF16)
        return dot(perm[...], both).astype(BF16)

    def from_rows(value):
        high = value.astype(BF16).astype(F32)
        both = jnp.concatenate([high, value - high], axis=1).astype(BF16)
        moved = dot(permt[...], both)
        moved = moved[:, :C] + moved[:, C:]
        return jnp.concatenate([moved[k * PM : (k + 1) * PM] for k in range(kk)], axis=1)

    lane = lax.broadcasted_iota(jnp.int32, (PM, half), 1)
    first_k = (gx * ngy + gy) % blocks * kk
    doubling = jnp.where(lane // C + first_k == 0, 1.0, 2.0).astype(F32)

    loads["field"].wait()
    loads["ybd"].wait()
    forward(0, vm["field"])
    for name in names:
        if name not in ("field", "ybd", "gz"):
            loads[name].wait()

    def iota(shape, dim):
        return lax.broadcasted_iota(jnp.int32, shape, dim)

    def fill(ref, make):
        one = make(iota(ref.shape, 0), iota(ref.shape, 1))
        ref[...] = jnp.where(one, 1.0, 0.0).astype(BF16)

    bits = kk.bit_length() - 1
    fill(perm, lambda r, c: c == (r & (kk - 1)) * PM + (r >> bits))
    fill(permt, lambda r, c: r == (c & (kk - 1)) * PM + (c >> bits))
    fill(ei, lambda r, c: (r & 31) == (c >> 5))
    fill(eo, lambda r, c: (r & 31) == (c & 31))
    fill(ro, lambda r, c: (r & 31) == c)
    fill(ri, lambda r, c: (r >> 5) == c)

    row = iota((256, C), 0) & 31
    col = iota((256, C), 1)
    sel = (row == col).astype(F32).astype(BF16)
    tall = dot(sel, vm["wp"][...]).astype(BF16)
    wide = lax.dot_general(tall, sel, (((1,), (1,)), ((), ())), preferred_element_type=F32)
    br = iota((256, 256), 0) >> 5
    bc = iota((256, 256), 1) >> 5
    kw[...] = jnp.where(br == bc, wide, 0.0).astype(BF16)
    bias = jnp.concatenate([vm["bias"][...]] * 8, axis=1)

    for b in range(4):
        at = slice(b * 256, b * 256 + 256)
        pre[:, at] = dot(vm["field"][:, at], kw[...]) + bias

    spec = gather_modes(0)

    vexp[...] = dot(to_rows(spec), ei[...])
    for m in range(KX):
        a, b = slice(m * kk, (m + 1) * kk), slice(n + m * kk, n + (m + 1) * kk)
        vr, vi = vexp[a], vexp[b]
        wr = vm["weight"][:, m * 2048 : m * 2048 + 1024].astype(F32)
        wi = vm["weight"][:, m * 2048 + 1024 : m * 2048 + 2048].astype(F32)
        pr = vr * wr - vi * wi
        pi = vr * wi + vi * wr
        red[a] = sum(pr[:, s * 128 : (s + 1) * 128] for s in range(8))
        red[b] = sum(pi[:, s * 128 : (s + 1) * 128] for s in range(8))
    high, low = split(red[...])
    out = dot(high, ro[...]) + dot(low, ro[...])
    scatter_modes(0, from_rows(out) * doubling)
    backward(0)

    @pl.loop(0, 4)
    def _(b):
        v = dot(vm["ybt"][...], gq[:, lanes(b)]) + pre[:, lanes(b)]
        root = math.sqrt(2.0 / math.pi)
        square = v * v
        th = jnp.tanh(root * v * (1.0 + 0.044715 * square))
        slope = 0.5 * (1.0 + th) + 0.5 * v * (1.0 - th * th) * (
            root * (1.0 + 3 * 0.044715 * square)
        )
        adj[:, lanes(b)] = (vm["cot"][:, lanes(b)].astype(F32) * slope).astype(BF16)

    forward(1, adj)

    acc[...] = jnp.zeros_like(acc)
    accb[...] = jnp.zeros_like(accb)
    ones = jnp.ones((16, rx * ry), BF16)

    @pl.loop(0, 4)
    def _(b):
        block = adj[:, lanes(b)]
        acc[...] += lax.dot_general(
            vm["field"][:, lanes(b)], block, (((0,), (0,)), ((), ())), preferred_element_type=F32
        )
        accb[...] += dot(ones, block)

    pbuf[...] = jnp.zeros_like(pbuf)
    pbuf[:C, :C] = sum(acc[i * C : (i + 1) * C, i * C : (i + 1) * C] for i in range(8)) * scale
    pbuf[C:, :C] = sum(accb[:8, i * C : (i + 1) * C] for i in range(8)) * scale
    for e in range(1, ngx):
        copy = pltpu.make_async_remote_copy(
            src_ref=pbuf,
            dst_ref=precv.at[gx],
            send_sem=p_send.at[e],
            recv_sem=p_recv.at[0],
            device_id={"gx": lax.rem(gx + e, ngx)},
            device_id_type=MESH,
        )
        copy.start()
        pending.append(copy)
    precv[gx] = pbuf[...]

    spec = gather_modes(1) * doubling
    hexp[...] = dot(to_rows(spec), eo[...])
    for m in range(KX):
        a, b = slice(m * kk, (m + 1) * kk), slice(n + m * kk, n + (m + 1) * kk)
        hr, hi = hexp[a], hexp[b]
        wr = vm["weight"][:, m * 2048 : m * 2048 + 1024].astype(F32)
        wi = vm["weight"][:, m * 2048 + 1024 : m * 2048 + 2048].astype(F32)
        prod[a] = hr * wr + hi * wi
        prod[b] = hi * wr - hr * wi
    high, low = split(prod[...])
    out = dot(high, ri[...]) + dot(low, ri[...])
    scatter_modes(1, from_rows(out))

    got = precv.at[pl.ds(0, ngx - 1)]
    pltpu.make_async_copy(got, got, p_recv.at[0]).wait()
    pbuf2[...] = sum(precv[i] for i in range(ngx))
    for d in range(1, ngy):
        copy = pltpu.make_async_remote_copy(
            src_ref=pbuf2,
            dst_ref=precv2.at[gy],
            send_sem=p_send.at[ngx + d],
            recv_sem=p_recv.at[1],
            device_id={"gy": lax.rem(gy + d, ngy)},
            device_id_type=MESH,
        )
        copy.start()
        pending.append(copy)
    precv2[gy] = pbuf2[...]

    for m in range(KX):
        a, b = slice(m * kk, (m + 1) * kk), slice(n + m * kk, n + (m + 1) * kk)
        vr, vi, hr, hi = vexp[a], vexp[b], hexp[a] * scale, hexp[b] * scale
        gs[:, m * 2048 : m * 2048 + 1024] = vr * hr + vi * hi
        gs[:, m * 2048 + 1024 : m * 2048 + 2048] = vr * hi - vi * hr
    gs_copy = pltpu.make_async_copy(gs, gs_out, gs_sem)
    gs_copy.start()

    backward(1)

    gf_copies = []
    for b in range(4):
        at = pl.ds(b * 256, 256)
        back = lax.dot_general(
            adj[:, at], kw[...], (((1,), (1,)), ((), ())), preferred_element_type=F32
        )
        gf[:, at] = (dot(vm["ybt"][...], gq[:, at]) + back).astype(BF16)
        gf_copies.append(pltpu.make_async_copy(gf.at[:, at], gf_out.at[:, at], gf_sem.at[b]))
        gf_copies[-1].start()

    got = precv2.at[pl.ds(0, ngy - 1)]
    pltpu.make_async_copy(got, got, p_recv.at[1]).wait()
    total = sum(precv2[i] for i in range(ngy))
    gp_out[...] = total[:C, :C]
    gb_out[...] = total[C : C + 1, :C]
    gs_copy.wait()
    for copy in gf_copies:
        copy.wait()
    for copy in pending:
        copy.wait_send()


def hand_over(*refs):
    sem = refs[-1]
    count = len(refs) // 2
    copies = []
    for i in range(count):
        copies.append(pltpu.make_async_copy(refs[i], refs[count + i], sem.at[i]))
        copies[-1].start()
    for copy in copies:
        copy.wait()


def on_device(ngx, ngy, field_input, cotangent, spectral_weight, point_weight, point_bias):
    rx, ry, depth = field_input.shape
    kk = spectral_weight.shape[0]
    cells = rx * ry
    nx = rx * ngx
    half, width = kk * C, 2 * kk * C
    arrays = dict(field=field_input.reshape(cells, depth))
    consts = tables(ngx, ngy, rx, ry, kk)
    arrays["ybd"] = consts["ybd"]
    arrays["gz"] = consts["gz"]
    arrays["xf"] = consts["xf"]
    arrays["weight"] = spectral_weight
    for name in TABLES:
        arrays[name] = consts[name]
    arrays["cot"] = cotangent.reshape(cells, depth)
    arrays["wp"] = point_weight
    arrays["bias"] = point_bias.reshape(1, C)
    names = tuple(arrays)
    local = [
        pltpu.VMEM(a.shape[1:] if k in BY_GY else a.shape, a.dtype) for k, a in arrays.items()
    ]
    rows = KY * rx
    n2 = PM * kk
    vmem = pl.BlockSpec(memory_space=pltpu.VMEM)
    hbm = pl.BlockSpec(memory_space=pl.ANY)
    dma = pltpu.SemaphoreType.DMA
    results = pl.pallas_call(
        functools.partial(kernel, ngx, ngy, rx, ry, kk, names),
        out_shape=(
            jax.ShapeDtypeStruct((cells, depth), BF16),
            jax.ShapeDtypeStruct(spectral_weight.shape, F32),
            jax.ShapeDtypeStruct((C, C), F32),
            jax.ShapeDtypeStruct((1, C), F32),
        ),
        in_specs=[pl.BlockSpec(memory_space=pltpu.HBM)] * len(names),
        out_specs=(hbm, hbm, vmem, vmem),
        scratch_shapes=local
        + [
            pltpu.VMEM((2 * rows, depth), BF16),
            pltpu.VMEM((2, rows, depth), F32),
            pltpu.VMEM((2, ngy, nx, width), F32),
            pltpu.VMEM((2, ngy, PM, half), F32),
            pltpu.VMEM((2, ngy, PM, half), F32),
            pltpu.VMEM((2, PM, half), F32),
            pltpu.VMEM((2, ngy, PM, half), F32),
            pltpu.VMEM((2, ngy, nx, width), F32),
            pltpu.VMEM((2, rows, depth), F32),
            pltpu.VMEM((2 * rows, depth), BF16),
            pltpu.VMEM((n2, C * C), F32),
            pltpu.VMEM((n2, C * C), F32),
            pltpu.VMEM((n2, 128), F32),
            pltpu.VMEM((n2, C * C), F32),
            pltpu.VMEM((cells, depth), BF16),
            pltpu.VMEM(spectral_weight.shape, F32),
            pltpu.VMEM((256, 256), F32),
            pltpu.VMEM((16, 256), F32),
            pltpu.VMEM((256, 256), BF16),
            pltpu.VMEM((C + 8, 128), F32),
            pltpu.VMEM((ngx, C + 8, 128), F32),
            pltpu.VMEM((C + 8, 128), F32),
            pltpu.VMEM((ngy, C + 8, 128), F32),
            pltpu.VMEM((2 * rows, KZ * C), BF16),
            pltpu.VMEM((cells, depth), F32),
            pltpu.VMEM((cells, depth), BF16),
            pltpu.VMEM((n2, n2), BF16),
            pltpu.VMEM((n2, n2), BF16),
            pltpu.VMEM((2 * C, C * C), BF16),
            pltpu.VMEM((2 * C, C * C), BF16),
            pltpu.VMEM((128, C), BF16),
            pltpu.VMEM((C * C, C), BF16),
            dma((len(names),)),
            dma,
            dma((4,)),
            dma((2, ngy, ngx - 1)),
            dma((2, ngy)),
            dma((2, ngy)),
            dma((2,)),
            dma((2, ngy)),
            dma((2, ngy)),
            dma((2, ngy, ngx - 1)),
            dma((2,)),
            dma((ngx + ngy,)),
            dma((2,)),
        ],
        compiler_params=pltpu.CompilerParams(
            collective_id=0, has_side_effects=True, vmem_limit_bytes=52 * 1024 * 1024
        ),
    )(*arrays.values())
    grad_field, grad_spectral, grad_point, grad_bias = pl.pallas_call(
        hand_over,
        out_shape=tuple(jax.ShapeDtypeStruct(r.shape, r.dtype) for r in results),
        in_specs=[hbm] * 4,
        out_specs=(hbm,) * 4,
        scratch_shapes=[dma((4,))],
    )(*results)
    return (
        grad_field.reshape(rx, ry, depth),
        grad_spectral,
        grad_point,
        grad_bias.reshape(C),
    )


def solution(mesh):
    return jax.shard_map(
        functools.partial(on_device, mesh.shape["gx"], mesh.shape["gy"]),
        mesh=mesh,
        in_specs=(
            P(("groups", "gx"), "gy", None),
            P(("groups", "gx"), "gy", None),
            P(("gx", "gy"), None),
            P(),
            P(),
        ),
        out_specs=(
            P(("groups", "gx"), "gy", None),
            P(("groups", "gx", "gy"), None),
            P("groups", None),
            P("groups"),
        ),
        check_vma=False,
    )
```

```python
import functools
import math

import jax
import jax.numpy as jnp
import numpy as np
from jax import lax
from jax.experimental import pallas as pl
from jax.experimental.pallas import tpu as pltpu
from jax.sharding import PartitionSpec as P

C = 32
KX = 16
KY = 16
KZ = 16
NZ = 32
PM = 2 * KX
F32 = jnp.float32
BF16 = jnp.bfloat16
MESH = pl.DeviceIdType.MESH


def modes(count, length):
    position = np.arange(count)
    return np.where(position < count // 2, position, length - count + position)


def angles(positions, wavenumbers, length):
    steps = positions[:, None] * wavenumbers[None, :] % length
    return 2.0 * math.pi / length * steps.astype(np.float64)


def tables(ngx, ngy, rows_x, rows_y, kk):
    full_x, full_y = ngx * rows_x, ngy * rows_y
    scale = 1.0 / math.sqrt(full_x * full_y * NZ)
    tz = angles(np.arange(NZ), np.arange(KZ), NZ)
    eye = np.eye(C, dtype=np.float32)
    to_modes = np.concatenate(
        [np.kron(f(tz).astype(np.float32), eye) for f in (np.cos, np.sin)], 1
    )
    from_modes = np.concatenate(
        [np.kron(f(tz).astype(np.float32).T, eye) for f in (np.cos, np.sin)], 1
    )
    ty = angles(np.arange(full_y), modes(KY, full_y), full_y).reshape(ngy, rows_y, KY)
    ytab = np.stack([np.cos(ty), -np.sin(ty)], 1).transpose(0, 1, 3, 2)
    ybd = np.einsum("gqjy,xw->gqjxwy", ytab, np.eye(rows_x))
    ybd = ybd.reshape(ngy, 2 * KY * rows_x, rows_x * rows_y)
    tx = angles(np.arange(full_x), modes(KX, full_x), full_x).T
    cx, sx = np.cos(tx) * scale, np.sin(tx) * scale
    xf = np.concatenate(
        [np.concatenate([cx, sx], 1), np.concatenate([-sx, cx], 1)], 0
    )
    bf = lambda a: np.ascontiguousarray(a).astype(jnp.bfloat16)

    def three(a):
        high = bf(a)
        low = bf(a - high.astype(np.float64))
        wide = np.concatenate([high, high, low], 1)
        return np.pad(wide, ((0, -len(wide) % 16), (0, to_modes.shape[1] - wide.shape[1])))

    return dict(
        ybd=jnp.asarray(bf(ybd)),
        gz=jnp.asarray(np.concatenate([bf(to_modes), three(xf), three(xf.T)], 0)),
        ybt=jnp.asarray(bf(ybd.transpose(0, 2, 1))),
        hz=jnp.asarray(bf(from_modes)),
    )


TABLES = ["ybd", "gz", "hz"]
BY_GY = ("ybd", "ybt")
VMEM_LIMIT = 61 * 1024 * 1024


def dot(a, b):
    return jnp.dot(a, b, preferred_element_type=F32)


def dot3(table, b):
    high, low = split(b)
    return dot(table, jnp.concatenate([high, low, high], axis=0))


def split(a):
    high = a.astype(BF16)
    return high, (a - high.astype(F32)).astype(BF16)


def iota(shape, dim):
    return lax.broadcasted_iota(jnp.int32, shape, dim)


def fill(ref, make):
    one = make(iota(ref.shape, 0), iota(ref.shape, 1))
    ref[...] = jnp.where(one, 1.0, 0.0).astype(BF16)


def over_out(r, c):
    return (r & 31) == (c >> 5)


def over_in(r, c):
    return (r & 31) == (c & 31)


def kernel(ngx, ngy, rx, ry, kk, parts, names, *refs):
    it = iter(refs)
    hbm = {name: next(it) for name in names}
    vr_out, hr_out, gq_out, adj_out, kw_out, tot_out = (next(it) for _ in range(6))
    vm = {name: next(it) for name in names}
    (ybuf, zout, recv1, send2, recv2, zs, recvs, fs, fin, gq, vexp, hexp, red, prod,
     adj, vrow, hrow, acc, accb, kw, pbuf, precv, pbuf2, precv2, f2, pre, gacc, tot, wf,
     perm, permt, ei, eo, ro, ri) = (next(it) for _ in range(35))
    (in_sem, out_sem, s1_send, s1_recv, s2_send, s2_recv, g_send, g_recv, f_send, f_recv,
     p_send, p_recv) = (next(it) for _ in range(12))

    gx, gy = lax.axis_index("gx"), lax.axis_index("gy")
    nx = ngx * rx
    kc = kk // parts
    half = kc * C
    width = 2 * half
    blocks = KZ // kc
    shares = KZ // kk
    n = KX * kc
    modes_in = KZ * C
    xf0, xs0 = NZ * C, NZ * C + PM
    scale = 1.0 / math.sqrt(nx * ngy * ry * NZ)

    loads = {}
    for i, name in enumerate(names):
        src = hbm[name].at[gy] if name in BY_GY else hbm[name]
        loads[name] = pltpu.make_async_copy(src, vm[name], in_sem.at[i])
        loads[name].start()

    barrier = pltpu.get_barrier_semaphore()
    for e in range(1, ngx):
        pl.semaphore_signal(barrier, inc=1, device_id={"gx": lax.rem(gx + e, ngx)}, device_id_type=MESH)
    for d in range(1, ngy):
        pl.semaphore_signal(barrier, inc=1, device_id={"gy": lax.rem(gy + d, ngy)}, device_id_type=MESH)

    def slab(ref, owner, h):
        rows = pl.ds(pl.multiple_of(owner // shares * rx, rx), rx)
        if shares == 1:
            return ref.at[rows, pl.ds(h * width, width)]
        block = owner % shares * parts + h
        return ref.at[rows, pl.ds(pl.multiple_of(block * width, width), width)]

    def lanes(b):
        return pl.ds(pl.multiple_of(b * 256, 256), 256)

    chips = ngx // 2
    chip, core = gx // 2, gx % 2
    steps = [(c, k) for c in range(1, chips) for k in range(2)] + [(0, 1)]
    peers = [lax.rem(chip + c, chips) * 2 + lax.rem(core + k, 2) for c, k in steps]
    way = 1 - 2 * (gy // (ngy // 2))

    def along(d):
        return lax.rem(gy + way * d + ngy, ngy)

    far_first = list(range(ngy - 1, -1, -1))
    pending = []

    rows = KY * rx

    def forward(t, u):
        for b in range(4):
            at = slice(b * 256, b * 256 + 256)
            ybuf[:, at] = dot(vm["ybd"][...], u[:, at]).astype(BF16)
        if t == 0:
            loads["gz"].wait()
        for b in range(2):
            cos = dot(ybuf[...], vm["gz"][: NZ * C, b * 256 : b * 256 + 256])
            sin = dot(ybuf[...], vm["gz"][: NZ * C, modes_in + b * 256 : modes_in + b * 256 + 256])
            real = cos[:rows] + sin[rows:]
            imag = cos[rows:] - sin[:rows]
            part = min(half, 256)
            for i in range(256 // part):
                lane0 = b * 256 + i * part
                at = lane0 // half * width + lane0 % half
                zout[t, :, at : at + part] = real[:, i * part : (i + 1) * part]
                zout[t, :, at + half : at + half + part] = imag[:, i * part : (i + 1) * part]
            if t == 0 and b == 0:
                pl.semaphore_wait(barrier, ngx + ngy - 2)
            if parts == 2:
                send_cells(t, b)
        if parts == 1:
            send_cells(t, 0)

    mine = pl.ds(pl.multiple_of(gx * rx, rx), rx)

    def send_cells(t, h):
        for d in far_first:
            g = along(d)
            for e, to in enumerate(peers):
                copy = pltpu.make_async_remote_copy(
                    src_ref=slab(zout.at[t], to * ngy + g, h),
                    dst_ref=recv1.at[t, h, g, mine],
                    send_sem=s1_send.at[t, h, d, e],
                    recv_sem=s1_recv.at[t, h, g],
                    device_id={"gx": to},
                    device_id_type=MESH,
                )
                copy.start()
                pending.append(copy)
            recv1[t, h, g, mine] = slab(zout.at[t], gx * ngy + g, h)[...]

    def send_sums(t, h):
        for d in far_first:
            g = along(d)
            got = recv1.at[t, h, g, pl.ds(0, (ngx - 1) * rx)]
            pltpu.make_async_copy(got, got, s1_recv.at[t, h, g]).wait()
            both = jnp.concatenate([recv1[t, h, g, :, :half], recv1[t, h, g, :, half:]], axis=0)
            value = dot3(vm["gz"][xf0 : xf0 + PM, : 6 * nx], both)
            if d == 0:
                recv2[t, h, gy] = value
            else:
                send2[t, h, d] = value
                copy = pltpu.make_async_remote_copy(
                    src_ref=send2.at[t, h, d],
                    dst_ref=recv2.at[t, h, gy],
                    send_sem=s2_send.at[t, h, d],
                    recv_sem=s2_recv.at[t, h],
                    device_id={"gy": g},
                    device_id_type=MESH,
                )
                copy.start()
                pending.append(copy)

    def add_sums(t, h):
        got = recv2.at[t, h, pl.ds(0, ngy - 1)]
        pltpu.make_async_copy(got, got, s2_recv.at[t, h]).wait()
        total = recv2[t, h, 0]
        for g in range(1, ngy):
            total = total + recv2[t, h, g]
        return total

    def send_modes(t, h, value):
        zs[t, h] = value
        for d in range(ngy - 1, 0, -1):
            copy = pltpu.make_async_remote_copy(
                src_ref=zs.at[t, h],
                dst_ref=recvs.at[t, h, gy],
                send_sem=g_send.at[t, h, d],
                recv_sem=g_recv.at[t, h, gy],
                device_id={"gy": along(d)},
                device_id_type=MESH,
            )
            copy.start()
            pending.append(copy)
        return_cells(t, h, 0, value)

    def return_cells(t, h, d, block):
        g = along(d)
        if d:
            got = recvs.at[t, h, g]
            pltpu.make_async_copy(got, got, g_recv.at[t, h, g]).wait()
            block = recvs[t, h, g]
        both = dot3(vm["gz"][xs0 : xs0 + 2 * nx, : 3 * PM], block)
        fs[t, h, g, :, :half] = both[:nx]
        fs[t, h, g, :, half:] = both[nx:]
        owner = gx * ngy + g
        for e, to in enumerate(peers):
            copy = pltpu.make_async_remote_copy(
                src_ref=fs.at[t, h, g, pl.ds(pl.multiple_of(to * rx, rx), rx)],
                dst_ref=slab(fin.at[t], owner, h),
                send_sem=f_send.at[t, h, d, e],
                recv_sem=f_recv.at[t, h],
                device_id={"gx": to},
                device_id_type=MESH,
            )
            copy.start()
            pending.append(copy)
        slab(fin.at[t], owner, h)[...] = fs[t, h, g, mine]

    def exchange(t, mix):
        for h in range(parts):
            send_sums(t, h)
        for h in range(parts):
            send_modes(t, h, mix(h, add_sums(t, h)))
        for h in range(parts):
            for d in range(1, ngy):
                return_cells(t, h, d, None)

    def backward(t):
        per = modes_in // parts
        for h in range(parts):
            got = fin.at[t, pl.ds(0, rows // ngx * (ngx - 1)), pl.ds(h * 2 * per, 2 * per)]
            pltpu.make_async_copy(got, got, f_recv.at[t, h]).wait()
            for kb in range(h * blocks // parts, (h + 1) * blocks // parts):
                at, to = kb * width, slice(kb * half, (kb + 1) * half)
                f2[:rows, to] = fin[t, :, at : at + half].astype(BF16)
                f2[rows:, to] = fin[t, :, at + half : at + width].astype(BF16)
            k = slice(h * per, (h + 1) * per)
            for b in range(4):
                at = slice(b * 256, b * 256 + 256)
                cos = dot(f2[:, k], vm["hz"][k, at])
                sin = dot(f2[:, k], vm["hz"][k, NZ * C + b * 256 : NZ * C + b * 256 + 256])
                real, imag = cos[:rows] - sin[rows:], sin[:rows] + cos[rows:]
                if h:
                    real, imag = real + gacc[:rows, at], imag + gacc[rows:, at]
                if h == parts - 1:
                    gq[:rows, at] = real.astype(BF16)
                    gq[rows:, at] = imag.astype(BF16)
                else:
                    gacc[:rows, at] = real
                    gacc[rows:, at] = imag

    def to_rows(value):
        stack = jnp.concatenate([value[:, k * C : (k + 1) * C] for k in range(kc)], axis=0)
        high = stack.astype(BF16).astype(F32)
        both = jnp.concatenate([high, stack - high], axis=1).astype(BF16)
        return dot(perm[...], both).astype(BF16)

    def from_rows(value):
        high = value.astype(BF16).astype(F32)
        both = jnp.concatenate([high, value - high], axis=1).astype(BF16)
        moved = dot(permt[...], both)
        moved = moved[:, :C] + moved[:, C:]
        return jnp.concatenate([moved[k * PM : (k + 1) * PM] for k in range(kc)], axis=1)

    lane = iota((PM, half), 1)
    first_k = (gx * ngy + gy) % shares * kk

    def doubling(h):
        return jnp.where((lane >> 5) + first_k + h * kc == 0, 1.0, 2.0).astype(F32)

    loads["field"].wait()
    loads["ybd"].wait()
    forward(0, vm["field"])
    for name in names:
        if name not in ("field", "ybd", "gz"):
            loads[name].wait()

    bits = kc.bit_length() - 1
    fill(perm, lambda r, c: c == (r & (kc - 1)) * PM + (r >> bits))
    fill(permt, lambda r, c: r == (c & (kc - 1)) * PM + (c >> bits))
    fill(ei, over_out)
    fill(eo, over_in)
    fill(ro, lambda r, c: (r & 31) == c)
    fill(ri, lambda r, c: (r >> 5) == c)

    row = iota((256, C), 0) & 31
    col = iota((256, C), 1)
    sel = (row == col).astype(F32).astype(BF16)
    tall = dot(sel, vm["wp"][...]).astype(BF16)
    wide = lax.dot_general(tall, sel, (((1,), (1,)), ((), ())), preferred_element_type=F32)
    br = iota((256, 256), 0) >> 5
    bc = iota((256, 256), 1) >> 5
    kw[...] = jnp.where(br == bc, wide, 0.0).astype(BF16)
    bias = jnp.concatenate([vm["bias"][...]] * 8, axis=1)

    for b in range(4):
        at = slice(b * 256, b * 256 + 256)
        pre[:, at] = dot(vm["field"][:, at], kw[...]) + bias

    for i in range(2 * KX):
        at = slice(i * C * C, (i + 1) * C * C)
        wf[:, at] = vm["weight"][:, at].astype(F32)

    def weights(h, m):
        k = slice(h * kc, (h + 1) * kc)
        return wf[k, m * 2048 : m * 2048 + 1024], wf[k, m * 2048 + 1024 : m * 2048 + 2048]

    def pair(m):
        return slice(m * kc, (m + 1) * kc), slice(n + m * kc, n + (m + 1) * kc)

    def mix_out(h, spec):
        vrow[h] = to_rows(spec)
        vexp[...] = dot(vrow[h], ei[...])
        for m in range(KX):
            a, b = pair(m)
            vr, vi = vexp[a], vexp[b]
            wr, wi = weights(h, m)
            pr = vr * wr - vi * wi
            pi = vr * wi + vi * wr
            red[a] = sum(pr[:, s * 128 : (s + 1) * 128] for s in range(8))
            red[b] = sum(pi[:, s * 128 : (s + 1) * 128] for s in range(8))
        high, low = split(red[...])
        out = dot(high, ro[...]) + dot(low, ro[...])
        return from_rows(out) * doubling(h)

    def mix_in(h, spec):
        hrow[h] = to_rows(spec * doubling(h))
        hexp[...] = dot(hrow[h], eo[...])
        for m in range(KX):
            a, b = pair(m)
            hr, hi = hexp[a], hexp[b]
            wr, wi = weights(h, m)
            prod[a] = hr * wr + hi * wi
            prod[b] = hi * wr - hr * wi
        high, low = split(prod[...])
        out = dot(high, ri[...]) + dot(low, ri[...])
        return from_rows(out)

    results = []

    def give(src, dst):
        results.append(pltpu.make_async_copy(src, dst, out_sem.at[len(results)]))
        results[-1].start()

    give(kw, kw_out)
    exchange(0, mix_out)
    give(vrow, vr_out)
    backward(0)

    @pl.loop(0, 4)
    def _(b):
        v = dot(vm["ybt"][...], gq[:, lanes(b)]) + pre[:, lanes(b)]
        root = math.sqrt(2.0 / math.pi)
        square = v * v
        th = jnp.tanh(root * v * (1.0 + 0.044715 * square))
        slope = 0.5 * (1.0 + th) + 0.5 * v * (1.0 - th * th) * (
            root * (1.0 + 3 * 0.044715 * square)
        )
        adj[:, lanes(b)] = (vm["cot"][:, lanes(b)].astype(F32) * slope).astype(BF16)

    give(adj, adj_out)
    forward(1, adj)

    acc[...] = jnp.zeros_like(acc)
    accb[...] = jnp.zeros_like(accb)
    ones = jnp.ones((16, rx * ry), BF16)

    @pl.loop(0, 4)
    def _(b):
        block = adj[:, lanes(b)]
        acc[...] += lax.dot_general(
            vm["field"][:, lanes(b)], block, (((0,), (0,)), ((), ())), preferred_element_type=F32
        )
        accb[...] += dot(ones, block)

    pbuf[...] = jnp.zeros_like(pbuf)
    pbuf[:C, :C] = sum(acc[i * C : (i + 1) * C, i * C : (i + 1) * C] for i in range(8)) * scale
    pbuf[C:, :C] = sum(accb[:8, i * C : (i + 1) * C] for i in range(8)) * scale
    for e in range(1, ngx):
        copy = pltpu.make_async_remote_copy(
            src_ref=pbuf,
            dst_ref=precv.at[gx],
            send_sem=p_send.at[e],
            recv_sem=p_recv.at[0],
            device_id={"gx": lax.rem(gx + e, ngx)},
            device_id_type=MESH,
        )
        copy.start()
        pending.append(copy)
    precv[gx] = pbuf[...]

    exchange(1, mix_in)
    give(hrow, hr_out)

    got = precv.at[pl.ds(0, ngx - 1)]
    pltpu.make_async_copy(got, got, p_recv.at[0]).wait()
    pbuf2[...] = sum(precv[i] for i in range(ngx))
    for d in range(1, ngy):
        copy = pltpu.make_async_remote_copy(
            src_ref=pbuf2,
            dst_ref=precv2.at[gy],
            send_sem=p_send.at[ngx + d],
            recv_sem=p_recv.at[1],
            device_id={"gy": lax.rem(gy + d, ngy)},
            device_id_type=MESH,
        )
        copy.start()
        pending.append(copy)
    precv2[gy] = pbuf2[...]

    backward(1)
    give(gq, gq_out)
    got = precv2.at[pl.ds(0, ngy - 1)]
    pltpu.make_async_copy(got, got, p_recv.at[1]).wait()
    tot[...] = sum(precv2[i] for i in range(ngy))
    give(tot, tot_out)
    for copy in results:
        copy.wait()
    for copy in pending:
        copy.wait_send()


def finish(scale, kk, parts, *refs):
    (vr_in, hr_in, gq_in, adj_in, kw_in, tot_in, ybt_in, gf_out, gs_out, gp_out, gb_out,
     vrow, hrow, gq, adj, kw, tot, ybt, gf, gs, gp, gb, vexp, hexp, ei, eo, in_sem,
     out_sem) = refs
    kc = kk // parts
    n = KX * kc
    loads = [
        pltpu.make_async_copy(src, dst, in_sem.at[i])
        for i, (src, dst) in enumerate(
            [(vr_in, vrow), (hr_in, hrow), (gq_in, gq), (adj_in, adj), (kw_in, kw),
             (tot_in, tot), (ybt_in.at[lax.axis_index("gy")], ybt)]
        )
    ]
    for load in loads:
        load.start()
    fill(ei, over_out)
    fill(eo, over_in)
    results = []

    def give(src, dst):
        results.append(pltpu.make_async_copy(src, dst, out_sem.at[len(results)]))
        results[-1].start()

    loads[0].wait()
    loads[1].wait()
    for h in range(parts):
        k = slice(h * kc, (h + 1) * kc)
        vexp[...] = dot(vrow[h], ei[...])
        hexp[...] = dot(hrow[h], eo[...])
        for m in range(KX):
            a, b = slice(m * kc, (m + 1) * kc), slice(n + m * kc, n + (m + 1) * kc)
            vr, vi, hr, hi = vexp[a], vexp[b], hexp[a] * scale, hexp[b] * scale
            gs[k, m * 2048 : m * 2048 + 1024] = vr * hr + vi * hi
            gs[k, m * 2048 + 1024 : m * 2048 + 2048] = vr * hi - vi * hr
        if parts == 1:
            give(gs, gs_out)
        else:
            give(gs.at[pl.ds(h * kc, kc)], gs_out.at[pl.ds(h * kc, kc)])
    for load in loads[2:]:
        load.wait()
    gp[...] = tot[:C, :C]
    gb[...] = tot[C : C + 1, :C]
    give(gp, gp_out)
    give(gb, gb_out)
    for b in range(4):
        at = pl.ds(b * 256, 256)
        back = lax.dot_general(
            adj[:, at], kw[...], (((1,), (1,)), ((), ())), preferred_element_type=F32
        )
        gf[:, at] = (dot(ybt[...], gq[:, at]) + back).astype(BF16)
        give(gf.at[:, at], gf_out.at[:, at])
    for copy in results:
        copy.wait()


def on_device(ngx, ngy, field_input, cotangent, spectral_weight, point_weight, point_bias):
    rx, ry, depth = field_input.shape
    kk = spectral_weight.shape[0]
    cells = rx * ry
    nx = rx * ngx
    parts = 2 if kk == KZ else 1
    kc = kk // parts
    half, width = kc * C, 2 * kc * C
    arrays = dict(field=field_input.reshape(cells, depth))
    consts = tables(ngx, ngy, rx, ry, kk)
    arrays["ybd"] = consts["ybd"]
    arrays["gz"] = consts["gz"]
    arrays["weight"] = spectral_weight
    for name in TABLES:
        arrays[name] = consts[name]
    arrays["ybt"] = consts["ybt"]
    arrays["cot"] = cotangent.reshape(cells, depth)
    arrays["wp"] = point_weight
    arrays["bias"] = point_bias.reshape(1, C)
    names = tuple(arrays)
    local = [
        pltpu.VMEM(a.shape[1:] if k in BY_GY else a.shape, a.dtype) for k, a in arrays.items()
    ]
    rows = KY * rx
    n2 = PM * kc
    hbm = pl.BlockSpec(memory_space=pltpu.HBM)
    dma = pltpu.SemaphoreType.DMA
    rows_type = jax.ShapeDtypeStruct((parts, n2, 2 * C), BF16)
    between = (
        rows_type,
        rows_type,
        jax.ShapeDtypeStruct((2 * rows, depth), BF16),
        jax.ShapeDtypeStruct((cells, depth), BF16),
        jax.ShapeDtypeStruct((256, 256), BF16),
        jax.ShapeDtypeStruct((C + 8, 128), F32),
    )

    def room(types):
        return [pltpu.VMEM(a.shape, a.dtype) for a in types]

    kept = pl.pallas_call(
        functools.partial(kernel, ngx, ngy, rx, ry, kk, parts, names),
        out_shape=between,
        in_specs=[hbm] * len(names),
        out_specs=(hbm,) * len(between),
        scratch_shapes=local
        + [
            pltpu.VMEM((2 * rows, depth), BF16),
            pltpu.VMEM((2, rows, depth), F32),
            pltpu.VMEM((2, parts, ngy, nx, width), F32),
            pltpu.VMEM((2, parts, ngy, PM, half), F32),
            pltpu.VMEM((2, parts, ngy, PM, half), F32),
            pltpu.VMEM((2, parts, PM, half), F32),
            pltpu.VMEM((2, parts, ngy, PM, half), F32),
            pltpu.VMEM((2, parts, ngy, nx, width), F32),
            pltpu.VMEM((2, rows, depth), F32),
            pltpu.VMEM((2 * rows, depth), BF16),
            pltpu.VMEM((n2, C * C), F32),
            pltpu.VMEM((n2, C * C), F32),
            pltpu.VMEM((n2, 128), F32),
            pltpu.VMEM((n2, C * C), F32),
            pltpu.VMEM((cells, depth), BF16),
            pltpu.VMEM((parts, n2, 2 * C), BF16),
            pltpu.VMEM((parts, n2, 2 * C), BF16),
            pltpu.VMEM((256, 256), F32),
            pltpu.VMEM((16, 256), F32),
            pltpu.VMEM((256, 256), BF16),
            pltpu.VMEM((C + 8, 128), F32),
            pltpu.VMEM((ngx, C + 8, 128), F32),
            pltpu.VMEM((C + 8, 128), F32),
            pltpu.VMEM((ngy, C + 8, 128), F32),
            pltpu.VMEM((2 * rows, KZ * C), BF16),
            pltpu.VMEM((cells, depth), F32),
            pltpu.VMEM((2 * rows, depth), F32),
            pltpu.VMEM((C + 8, 128), F32),
            pltpu.VMEM(spectral_weight.shape, F32),
            pltpu.VMEM((n2, n2), BF16),
            pltpu.VMEM((n2, n2), BF16),
            pltpu.VMEM((2 * C, C * C), BF16),
            pltpu.VMEM((2 * C, C * C), BF16),
            pltpu.VMEM((128, C), BF16),
            pltpu.VMEM((C * C, C), BF16),
            dma((len(names),)),
            dma((len(between),)),
            dma((2, parts, ngy, ngx - 1)),
            dma((2, parts, ngy)),
            dma((2, parts, ngy)),
            dma((2, parts)),
            dma((2, parts, ngy)),
            dma((2, parts, ngy)),
            dma((2, parts, ngy, ngx - 1)),
            dma((2, parts)),
            dma((ngx + ngy,)),
            dma((2,)),
        ],
        compiler_params=pltpu.CompilerParams(
            collective_id=0, has_side_effects=True, vmem_limit_bytes=VMEM_LIMIT
        ),
    )(*arrays.values())
    wanted = (
        jax.ShapeDtypeStruct((cells, depth), BF16),
        jax.ShapeDtypeStruct(spectral_weight.shape, F32),
        jax.ShapeDtypeStruct((C, C), F32),
        jax.ShapeDtypeStruct((1, C), F32),
    )
    scale = 1.0 / math.sqrt(nx * ngy * ry * NZ)
    grad_field, grad_spectral, grad_point, grad_bias = pl.pallas_call(
        functools.partial(finish, scale, kk, parts),
        out_shape=wanted,
        in_specs=[hbm] * (len(between) + 1),
        out_specs=(hbm,) * len(wanted),
        scratch_shapes=room(between)
        + [pltpu.VMEM(consts["ybt"].shape[1:], BF16)]
        + room(wanted)
        + [
            pltpu.VMEM((n2, C * C), F32),
            pltpu.VMEM((n2, C * C), F32),
            pltpu.VMEM((2 * C, C * C), BF16),
            pltpu.VMEM((2 * C, C * C), BF16),
            dma((len(between) + 1,)),
            dma((parts + 6,)),
        ],
        compiler_params=pltpu.CompilerParams(vmem_limit_bytes=VMEM_LIMIT),
    )(*kept, consts["ybt"])
    return (
        grad_field.reshape(rx, ry, depth),
        grad_spectral,
        grad_point,
        grad_bias.reshape(C),
    )


def solution(mesh):
    return jax.shard_map(
        functools.partial(on_device, mesh.shape["gx"], mesh.shape["gy"]),
        mesh=mesh,
        in_specs=(
            P(("groups", "gx"), "gy", None),
            P(("groups", "gx"), "gy", None),
            P(("gx", "gy"), None),
            P(),
            P(),
        ),
        out_specs=(
            P(("groups", "gx"), "gy", None),
            P(("groups", "gx", "gy"), None),
            P("groups", None),
            P("groups"),
        ),
        check_vma=False,
    )
```

```python
import functools
import math

import jax
import jax.numpy as jnp
import numpy as np
from jax import lax
from jax.experimental import pallas as pl
from jax.experimental.pallas import tpu as pltpu
from jax.sharding import PartitionSpec as P

C = 32
KX = 16
KY = 16
KZ = 16
NZ = 32
PM = 2 * KX
F32 = jnp.float32
BF16 = jnp.bfloat16
MESH = pl.DeviceIdType.MESH


def modes(count, length):
    position = np.arange(count)
    return np.where(position < count // 2, position, length - count + position)


def angles(positions, wavenumbers, length):
    steps = positions[:, None] * wavenumbers[None, :] % length
    return 2.0 * math.pi / length * steps.astype(np.float64)


def tables(ngx, ngy, rows_x, rows_y, kk):
    full_x, full_y = ngx * rows_x, ngy * rows_y
    scale = 1.0 / math.sqrt(full_x * full_y * NZ)
    tz = angles(np.arange(NZ), np.arange(KZ), NZ)
    eye = np.eye(C, dtype=np.float32)
    to_modes = np.concatenate(
        [np.kron(f(tz).astype(np.float32), eye) for f in (np.cos, np.sin)], 1
    )
    from_modes = np.concatenate(
        [np.kron(f(tz).astype(np.float32).T, eye) for f in (np.cos, np.sin)], 1
    )
    ty = angles(np.arange(full_y), modes(KY, full_y), full_y).reshape(ngy, rows_y, KY)
    ytab = np.stack([np.cos(ty), -np.sin(ty)], 1).transpose(0, 1, 3, 2)
    ybd = np.einsum("gqjy,xw->gqjxwy", ytab, np.eye(rows_x))
    ybd = ybd.reshape(ngy, 2 * KY * rows_x, rows_x * rows_y)
    tx = angles(np.arange(full_x), modes(KX, full_x), full_x).T
    cx, sx = np.cos(tx) * scale, np.sin(tx) * scale
    xf = np.concatenate(
        [np.concatenate([cx, sx], 1), np.concatenate([-sx, cx], 1)], 0
    )
    bf = lambda a: np.ascontiguousarray(a).astype(jnp.bfloat16)

    def three(a):
        high = bf(a)
        low = bf(a - high.astype(np.float64))
        wide = np.concatenate([high, high, low], 1)
        return np.pad(wide, ((0, -len(wide) % 16), (0, to_modes.shape[1] - wide.shape[1])))

    return dict(
        ybd=jnp.asarray(bf(ybd)),
        gz=jnp.asarray(np.concatenate([bf(to_modes), three(xf), three(xf.T)], 0)),
        ybt=jnp.asarray(bf(ybd.transpose(0, 2, 1))),
        hz=jnp.asarray(bf(from_modes)),
    )


TABLES = ["ybd", "gz", "hz"]
BY_GY = ("ybd", "ybt")
VMEM_LIMIT = 61 * 1024 * 1024


def dot(a, b):
    return jnp.dot(a, b, preferred_element_type=F32)


def dot3(table, b):
    high, low = split(b)
    return dot(table, jnp.concatenate([high, low, high], axis=0))


def split(a):
    high = a.astype(BF16)
    return high, (a - high.astype(F32)).astype(BF16)


def iota(shape, dim):
    return lax.broadcasted_iota(jnp.int32, shape, dim)


def fill(ref, make):
    one = make(iota(ref.shape, 0), iota(ref.shape, 1))
    ref[...] = jnp.where(one, 1.0, 0.0).astype(BF16)


def over_out(r, c):
    return (r & 31) == (c >> 5)


def over_in(r, c):
    return (r & 31) == (c & 31)


def kernel(ngx, ngy, rx, ry, kk, parts, names, *refs):
    it = iter(refs)
    hbm = {name: next(it) for name in names}
    vr_out, hr_out, gq_out, adj_out, kw_out, tot_out = (next(it) for _ in range(6))
    vm = {name: next(it) for name in names}
    (ybuf, zout, recv1, send2, recv2, zs, recvs, fs, fin, gq, vexp, hexp, red, prod,
     adj, vrow, hrow, acc, accb, kw, pbuf, precv, pbuf2, precv2, f2, pre, gacc, tot, wf,
     perm, permt, ei, eo, ro, ri) = (next(it) for _ in range(35))
    (in_sem, out_sem, s1_send, s1_recv, s2_send, s2_recv, g_send, g_recv, f_send, f_recv,
     p_send, p_recv) = (next(it) for _ in range(12))

    gx, gy = lax.axis_index("gx"), lax.axis_index("gy")
    nx = ngx * rx
    kc = kk // parts
    half = kc * C
    width = 2 * half
    blocks = KZ // kc
    shares = KZ // kk
    n = KX * kc
    modes_in = KZ * C
    xf0, xs0 = NZ * C, NZ * C + PM
    scale = 1.0 / math.sqrt(nx * ngy * ry * NZ)

    loads = {}
    for i, name in enumerate(names):
        src = hbm[name].at[gy] if name in BY_GY else hbm[name]
        loads[name] = pltpu.make_async_copy(src, vm[name], in_sem.at[i])
    early = ("field", "ybd", "gz")
    for name in early:
        loads[name].start()

    barrier = pltpu.get_barrier_semaphore()
    for e in range(1, ngx):
        pl.semaphore_signal(barrier, inc=1, device_id={"gx": lax.rem(gx + e, ngx)}, device_id_type=MESH)
    for d in range(1, ngy):
        pl.semaphore_signal(barrier, inc=1, device_id={"gy": lax.rem(gy + d, ngy)}, device_id_type=MESH)

    def slab(ref, owner, h):
        rows = pl.ds(pl.multiple_of(owner // shares * rx, rx), rx)
        if shares == 1:
            return ref.at[rows, pl.ds(h * width, width)]
        block = owner % shares * parts + h
        return ref.at[rows, pl.ds(pl.multiple_of(block * width, width), width)]

    chips = ngx // 2
    chip, core = gx // 2, gx % 2
    steps = [(c, k) for c in range(1, chips) for k in range(2)] + [(0, 1)]
    peers = [lax.rem(chip + c, chips) * 2 + lax.rem(core + k, 2) for c, k in steps]
    way = 1 - 2 * (gy // (ngy // 2))

    def along(d):
        return lax.rem(gy + way * d + ngy, ngy)

    far_first = list(range(ngy - 1, -1, -1))
    pending = []

    rows = KY * rx

    def forward(t):
        for b in range(2):
            cos = dot(ybuf[...], vm["gz"][: NZ * C, b * 256 : b * 256 + 256])
            sin = dot(ybuf[...], vm["gz"][: NZ * C, modes_in + b * 256 : modes_in + b * 256 + 256])
            real = cos[:rows] + sin[rows:]
            imag = cos[rows:] - sin[:rows]
            part = min(half, 256)
            for i in range(256 // part):
                lane0 = b * 256 + i * part
                at = lane0 // half * width + lane0 % half
                zout[t, :, at : at + part] = real[:, i * part : (i + 1) * part]
                zout[t, :, at + half : at + half + part] = imag[:, i * part : (i + 1) * part]
            if t == 0 and b == 0:
                pl.semaphore_wait(barrier, ngx + ngy - 2)
            if parts == 2:
                send_cells(t, b)
        if parts == 1:
            send_cells(t, 0)

    mine = pl.ds(pl.multiple_of(gx * rx, rx), rx)

    def send_cells(t, h):
        for d in far_first:
            g = along(d)
            for e, to in enumerate(peers):
                copy = pltpu.make_async_remote_copy(
                    src_ref=slab(zout.at[t], to * ngy + g, h),
                    dst_ref=recv1.at[t, h, g, mine],
                    send_sem=s1_send.at[t, h, d, e],
                    recv_sem=s1_recv.at[t, h, g],
                    device_id={"gx": to},
                    device_id_type=MESH,
                )
                copy.start()
                pending.append(copy)
            recv1[t, h, g, mine] = slab(zout.at[t], gx * ngy + g, h)[...]

    def send_sums(t, h):
        for d in far_first:
            g = along(d)
            got = recv1.at[t, h, g, pl.ds(0, (ngx - 1) * rx)]
            pltpu.make_async_copy(got, got, s1_recv.at[t, h, g]).wait()
            both = jnp.concatenate([recv1[t, h, g, :, :half], recv1[t, h, g, :, half:]], axis=0)
            value = dot3(vm["gz"][xf0 : xf0 + PM, : 6 * nx], both)
            if d == 0:
                recv2[t, h, gy] = value
            else:
                send2[t, h, d] = value
                copy = pltpu.make_async_remote_copy(
                    src_ref=send2.at[t, h, d],
                    dst_ref=recv2.at[t, h, gy],
                    send_sem=s2_send.at[t, h, d],
                    recv_sem=s2_recv.at[t, h],
                    device_id={"gy": g},
                    device_id_type=MESH,
                )
                copy.start()
                pending.append(copy)

    def add_sums(t, h):
        got = recv2.at[t, h, pl.ds(0, ngy - 1)]
        pltpu.make_async_copy(got, got, s2_recv.at[t, h]).wait()
        total = recv2[t, h, 0]
        for g in range(1, ngy):
            total = total + recv2[t, h, g]
        return total

    def send_modes(t, h, value):
        zs[t, h] = value
        for d in range(ngy - 1, 0, -1):
            copy = pltpu.make_async_remote_copy(
                src_ref=zs.at[t, h],
                dst_ref=recvs.at[t, h, gy],
                send_sem=g_send.at[t, h, d],
                recv_sem=g_recv.at[t, h, gy],
                device_id={"gy": along(d)},
                device_id_type=MESH,
            )
            copy.start()
            pending.append(copy)
        return_cells(t, h, 0, value)

    def return_cells(t, h, d, block):
        g = along(d)
        if d:
            got = recvs.at[t, h, g]
            pltpu.make_async_copy(got, got, g_recv.at[t, h, g]).wait()
            block = recvs[t, h, g]
        both = dot3(vm["gz"][xs0 : xs0 + 2 * nx, : 3 * PM], block)
        fs[t, h, g, :, :half] = both[:nx]
        fs[t, h, g, :, half:] = both[nx:]
        owner = gx * ngy + g
        for e, to in enumerate(peers):
            copy = pltpu.make_async_remote_copy(
                src_ref=fs.at[t, h, g, pl.ds(pl.multiple_of(to * rx, rx), rx)],
                dst_ref=slab(fin.at[t], owner, h),
                send_sem=f_send.at[t, h, d, e],
                recv_sem=f_recv.at[t, h],
                device_id={"gx": to},
                device_id_type=MESH,
            )
            copy.start()
            pending.append(copy)
        slab(fin.at[t], owner, h)[...] = fs[t, h, g, mine]

    def exchange(t, mix, beside):
        for h in range(parts):
            send_sums(t, h)
            if h == 0:
                beside()
        for h in range(parts):
            send_modes(t, h, mix(h, add_sums(t, h)))
        for h in range(parts):
            for d in range(1, ngy):
                return_cells(t, h, d, None)

    def backward(t, use):
        per = modes_in // parts
        for h in range(parts):
            got = fin.at[t, pl.ds(0, rows // ngx * (ngx - 1)), pl.ds(h * 2 * per, 2 * per)]
            pltpu.make_async_copy(got, got, f_recv.at[t, h]).wait()
            for kb in range(h * blocks // parts, (h + 1) * blocks // parts):
                at, to = kb * width, slice(kb * half, (kb + 1) * half)
                f2[:rows, to] = fin[t, :, at : at + half].astype(BF16)
                f2[rows:, to] = fin[t, :, at + half : at + width].astype(BF16)
            k = slice(h * per, (h + 1) * per)
            for b in range(4):
                at = slice(b * 256, b * 256 + 256)
                cos = dot(f2[:, k], vm["hz"][k, at])
                sin = dot(f2[:, k], vm["hz"][k, NZ * C + b * 256 : NZ * C + b * 256 + 256])
                real, imag = cos[:rows] - sin[rows:], sin[:rows] + cos[rows:]
                if h:
                    real, imag = real + gacc[:rows, at], imag + gacc[rows:, at]
                if h == parts - 1:
                    gq[:rows, at] = real.astype(BF16)
                    gq[rows:, at] = imag.astype(BF16)
                    use(at)
                else:
                    gacc[:rows, at] = real
                    gacc[rows:, at] = imag

    def to_rows(value):
        stack = jnp.concatenate([value[:, k * C : (k + 1) * C] for k in range(kc)], axis=0)
        high = stack.astype(BF16).astype(F32)
        both = jnp.concatenate([high, stack - high], axis=1).astype(BF16)
        return dot(perm[...], both).astype(BF16)

    def from_rows(value):
        high = value.astype(BF16).astype(F32)
        both = jnp.concatenate([high, value - high], axis=1).astype(BF16)
        moved = dot(permt[...], both)
        moved = moved[:, :C] + moved[:, C:]
        return jnp.concatenate([moved[k * PM : (k + 1) * PM] for k in range(kc)], axis=1)

    lane = iota((PM, half), 1)
    first_k = (gx * ngy + gy) % shares * kk

    def doubling(h):
        return jnp.where((lane >> 5) + first_k + h * kc == 0, 1.0, 2.0).astype(F32)

    loads["field"].wait()
    loads["ybd"].wait()
    for b in range(4):
        at = slice(b * 256, b * 256 + 256)
        ybuf[:, at] = dot(vm["ybd"][...], vm["field"][:, at]).astype(BF16)
    loads["gz"].wait()
    for name in names:
        if name not in early:
            loads[name].start()
    forward(0)
    for name in names:
        if name not in early:
            loads[name].wait()

    bits = kc.bit_length() - 1
    fill(perm, lambda r, c: c == (r & (kc - 1)) * PM + (r >> bits))
    fill(permt, lambda r, c: r == (c & (kc - 1)) * PM + (c >> bits))
    fill(ei, over_out)
    fill(eo, over_in)
    fill(ro, lambda r, c: (r & 31) == c)
    fill(ri, lambda r, c: (r >> 5) == c)

    row = iota((256, C), 0) & 31
    col = iota((256, C), 1)
    sel = (row == col).astype(F32).astype(BF16)
    tall = dot(sel, vm["wp"][...]).astype(BF16)
    wide = lax.dot_general(tall, sel, (((1,), (1,)), ((), ())), preferred_element_type=F32)
    br = iota((256, 256), 0) >> 5
    bc = iota((256, 256), 1) >> 5
    kw[...] = jnp.where(br == bc, wide, 0.0).astype(BF16)
    bias = jnp.concatenate([vm["bias"][...]] * 8, axis=1)

    def weights(h, m):
        k = slice(h * kc, (h + 1) * kc)
        return wf[k, m * 2048 : m * 2048 + 1024], wf[k, m * 2048 + 1024 : m * 2048 + 2048]

    def pair(m):
        return slice(m * kc, (m + 1) * kc), slice(n + m * kc, n + (m + 1) * kc)

    def mix_out(h, spec):
        vrow[h] = to_rows(spec)
        vexp[...] = dot(vrow[h], ei[...])
        for m in range(KX):
            a, b = pair(m)
            vr, vi = vexp[a], vexp[b]
            wr, wi = weights(h, m)
            pr = vr * wr - vi * wi
            pi = vr * wi + vi * wr
            red[a] = sum(pr[:, s * 128 : (s + 1) * 128] for s in range(8))
            red[b] = sum(pi[:, s * 128 : (s + 1) * 128] for s in range(8))
        high, low = split(red[...])
        out = dot(high, ro[...]) + dot(low, ro[...])
        return from_rows(out) * doubling(h)

    def mix_in(h, spec):
        hrow[h] = to_rows(spec * doubling(h))
        hexp[...] = dot(hrow[h], eo[...])
        for m in range(KX):
            a, b = pair(m)
            hr, hi = hexp[a], hexp[b]
            wr, wi = weights(h, m)
            prod[a] = hr * wr + hi * wi
            prod[b] = hi * wr - hr * wi
        high, low = split(prod[...])
        out = dot(high, ri[...]) + dot(low, ri[...])
        return from_rows(out)

    def widen():
        for i in range(2 * KX):
            at = slice(i * C * C, (i + 1) * C * C)
            wf[:, at] = vm["weight"][:, at].astype(F32)
        for b in range(4):
            at = slice(b * 256, b * 256 + 256)
            pre[:, at] = dot(vm["field"][:, at], kw[...]) + bias

    results = []

    def give(src, dst):
        results.append(pltpu.make_async_copy(src, dst, out_sem.at[len(results)]))
        results[-1].start()

    give(kw, kw_out)
    exchange(0, mix_out, widen)
    give(vrow, vr_out)

    def cell_work(at):
        v = dot(vm["ybt"][...], gq[:, at]) + pre[:, at]
        root = math.sqrt(2.0 / math.pi)
        square = v * v
        th = jnp.tanh(v * (root + (0.044715 * root) * square))
        slope = 0.5 * (1.0 + th) + v * (1.0 - th * th) * (
            0.5 * root + (1.5 * 0.044715 * root) * square
        )
        value = (vm["cot"][:, at].astype(F32) * slope).astype(BF16)
        adj[:, at] = value
        ybuf[:, at] = dot(vm["ybd"][...], value).astype(BF16)

    backward(0, cell_work)
    give(adj, adj_out)
    forward(1)

    def point_gradients():
        ones = jnp.ones((16, rx * ry), BF16)

        grad, total = 0.0, 0.0
        for b in range(4):
            at = slice(b * 256, b * 256 + 256)
            block = adj[:, at]
            grad += lax.dot_general(
                vm["field"][:, at], block, (((0,), (0,)), ((), ())), preferred_element_type=F32
            )
            total += dot(ones, block)
        acc[...] = grad
        accb[...] = total

        pbuf[...] = jnp.zeros_like(pbuf)
        pbuf[:C, :C] = sum(acc[i * C : (i + 1) * C, i * C : (i + 1) * C] for i in range(8)) * scale
        pbuf[C:, :C] = sum(accb[:8, i * C : (i + 1) * C] for i in range(8)) * scale
        for e in range(1, ngx):
            copy = pltpu.make_async_remote_copy(
                src_ref=pbuf,
                dst_ref=precv.at[gx],
                send_sem=p_send.at[e],
                recv_sem=p_recv.at[0],
                device_id={"gx": lax.rem(gx + e, ngx)},
                device_id_type=MESH,
            )
            copy.start()
            pending.append(copy)
        precv[gx] = pbuf[...]

    exchange(1, mix_in, point_gradients)
    give(hrow, hr_out)

    got = precv.at[pl.ds(0, ngx - 1)]
    pltpu.make_async_copy(got, got, p_recv.at[0]).wait()
    pbuf2[...] = sum(precv[i] for i in range(ngx))
    for d in range(1, ngy):
        copy = pltpu.make_async_remote_copy(
            src_ref=pbuf2,
            dst_ref=precv2.at[gy],
            send_sem=p_send.at[ngx + d],
            recv_sem=p_recv.at[1],
            device_id={"gy": lax.rem(gy + d, ngy)},
            device_id_type=MESH,
        )
        copy.start()
        pending.append(copy)
    precv2[gy] = pbuf2[...]

    backward(1, lambda at: None)
    give(gq, gq_out)
    got = precv2.at[pl.ds(0, ngy - 1)]
    pltpu.make_async_copy(got, got, p_recv.at[1]).wait()
    tot[...] = sum(precv2[i] for i in range(ngy))
    give(tot, tot_out)
    for copy in results:
        copy.wait()
    for copy in pending:
        copy.wait_send()


def finish(scale, kk, parts, *refs):
    (vr_in, hr_in, gq_in, adj_in, kw_in, tot_in, ybt_in, gf_out, gs_out, gp_out, gb_out,
     vrow, hrow, gq, adj, kw, tot, ybt, gf, gs, gp, gb, vexp, hexp, ei, eo, in_sem,
     out_sem) = refs
    kc = kk // parts
    n = KX * kc
    loads = [
        pltpu.make_async_copy(src, dst, in_sem.at[i])
        for i, (src, dst) in enumerate(
            [(vr_in, vrow), (hr_in, hrow), (gq_in, gq), (adj_in, adj), (kw_in, kw),
             (tot_in, tot), (ybt_in.at[lax.axis_index("gy")], ybt)]
        )
    ]
    for load in loads:
        load.start()
    fill(ei, over_out)
    fill(eo, over_in)
    results = []

    def give(src, dst):
        results.append(pltpu.make_async_copy(src, dst, out_sem.at[len(results)]))
        results[-1].start()

    loads[0].wait()
    loads[1].wait()
    for h in range(parts):
        k = slice(h * kc, (h + 1) * kc)
        vexp[...] = dot(vrow[h], ei[...])
        hexp[...] = dot(hrow[h], eo[...])
        for m in range(KX):
            a, b = slice(m * kc, (m + 1) * kc), slice(n + m * kc, n + (m + 1) * kc)
            vr, vi, hr, hi = vexp[a], vexp[b], hexp[a] * scale, hexp[b] * scale
            gs[k, m * 2048 : m * 2048 + 1024] = vr * hr + vi * hi
            gs[k, m * 2048 + 1024 : m * 2048 + 2048] = vr * hi - vi * hr
        if parts == 1:
            give(gs, gs_out)
        else:
            give(gs.at[pl.ds(h * kc, kc)], gs_out.at[pl.ds(h * kc, kc)])
    for load in loads[2:]:
        load.wait()
    gp[...] = tot[:C, :C]
    gb[...] = tot[C : C + 1, :C]
    give(gp, gp_out)
    give(gb, gb_out)
    for b in range(4):
        at = pl.ds(b * 256, 256)
        back = lax.dot_general(
            adj[:, at], kw[...], (((1,), (1,)), ((), ())), preferred_element_type=F32
        )
        gf[:, at] = (dot(ybt[...], gq[:, at]) + back).astype(BF16)
        give(gf.at[:, at], gf_out.at[:, at])
    for copy in results:
        copy.wait()


def on_device(ngx, ngy, field_input, cotangent, spectral_weight, point_weight, point_bias):
    rx, ry, depth = field_input.shape
    kk = spectral_weight.shape[0]
    cells = rx * ry
    nx = rx * ngx
    parts = 2 if kk == KZ else 1
    kc = kk // parts
    half, width = kc * C, 2 * kc * C
    arrays = dict(field=field_input.reshape(cells, depth))
    consts = tables(ngx, ngy, rx, ry, kk)
    arrays["ybd"] = consts["ybd"]
    arrays["gz"] = consts["gz"]
    arrays["weight"] = spectral_weight
    for name in TABLES:
        arrays[name] = consts[name]
    arrays["ybt"] = consts["ybt"]
    arrays["cot"] = cotangent.reshape(cells, depth)
    arrays["wp"] = point_weight
    arrays["bias"] = point_bias.reshape(1, C)
    names = tuple(arrays)
    local = [
        pltpu.VMEM(a.shape[1:] if k in BY_GY else a.shape, a.dtype) for k, a in arrays.items()
    ]
    rows = KY * rx
    n2 = PM * kc
    hbm = pl.BlockSpec(memory_space=pltpu.HBM)
    dma = pltpu.SemaphoreType.DMA
    rows_type = jax.ShapeDtypeStruct((parts, n2, 2 * C), BF16)
    between = (
        rows_type,
        rows_type,
        jax.ShapeDtypeStruct((2 * rows, depth), BF16),
        jax.ShapeDtypeStruct((cells, depth), BF16),
        jax.ShapeDtypeStruct((256, 256), BF16),
        jax.ShapeDtypeStruct((C + 8, 128), F32),
    )

    def room(types):
        return [pltpu.VMEM(a.shape, a.dtype) for a in types]

    kept = pl.pallas_call(
        functools.partial(kernel, ngx, ngy, rx, ry, kk, parts, names),
        out_shape=between,
        in_specs=[hbm] * len(names),
        out_specs=(hbm,) * len(between),
        scratch_shapes=local
        + [
            pltpu.VMEM((2 * rows, depth), BF16),
            pltpu.VMEM((2, rows, depth), F32),
            pltpu.VMEM((2, parts, ngy, nx, width), F32),
            pltpu.VMEM((2, parts, ngy, PM, half), F32),
            pltpu.VMEM((2, parts, ngy, PM, half), F32),
            pltpu.VMEM((2, parts, PM, half), F32),
            pltpu.VMEM((2, parts, ngy, PM, half), F32),
            pltpu.VMEM((2, parts, ngy, nx, width), F32),
            pltpu.VMEM((2, rows, depth), F32),
            pltpu.VMEM((2 * rows, depth), BF16),
            pltpu.VMEM((n2, C * C), F32),
            pltpu.VMEM((n2, C * C), F32),
            pltpu.VMEM((n2, 128), F32),
            pltpu.VMEM((n2, C * C), F32),
            pltpu.VMEM((cells, depth), BF16),
            pltpu.VMEM((parts, n2, 2 * C), BF16),
            pltpu.VMEM((parts, n2, 2 * C), BF16),
            pltpu.VMEM((256, 256), F32),
            pltpu.VMEM((16, 256), F32),
            pltpu.VMEM((256, 256), BF16),
            pltpu.VMEM((C + 8, 128), F32),
            pltpu.VMEM((ngx, C + 8, 128), F32),
            pltpu.VMEM((C + 8, 128), F32),
            pltpu.VMEM((ngy, C + 8, 128), F32),
            pltpu.VMEM((2 * rows, KZ * C), BF16),
            pltpu.VMEM((cells, depth), F32),
            pltpu.VMEM((2 * rows, depth), F32),
            pltpu.VMEM((C + 8, 128), F32),
            pltpu.VMEM(spectral_weight.shape, F32),
            pltpu.VMEM((n2, n2), BF16),
            pltpu.VMEM((n2, n2), BF16),
            pltpu.VMEM((2 * C, C * C), BF16),
            pltpu.VMEM((2 * C, C * C), BF16),
            pltpu.VMEM((128, C), BF16),
            pltpu.VMEM((C * C, C), BF16),
            dma((len(names),)),
            dma((len(between),)),
            dma((2, parts, ngy, ngx - 1)),
            dma((2, parts, ngy)),
            dma((2, parts, ngy)),
            dma((2, parts)),
            dma((2, parts, ngy)),
            dma((2, parts, ngy)),
            dma((2, parts, ngy, ngx - 1)),
            dma((2, parts)),
            dma((ngx + ngy,)),
            dma((2,)),
        ],
        compiler_params=pltpu.CompilerParams(
            collective_id=0, has_side_effects=True, vmem_limit_bytes=VMEM_LIMIT
        ),
    )(*arrays.values())
    wanted = (
        jax.ShapeDtypeStruct((cells, depth), BF16),
        jax.ShapeDtypeStruct(spectral_weight.shape, F32),
        jax.ShapeDtypeStruct((C, C), F32),
        jax.ShapeDtypeStruct((1, C), F32),
    )
    scale = 1.0 / math.sqrt(nx * ngy * ry * NZ)
    grad_field, grad_spectral, grad_point, grad_bias = pl.pallas_call(
        functools.partial(finish, scale, kk, parts),
        out_shape=wanted,
        in_specs=[hbm] * (len(between) + 1),
        out_specs=(hbm,) * len(wanted),
        scratch_shapes=room(between)
        + [pltpu.VMEM(consts["ybt"].shape[1:], BF16)]
        + room(wanted)
        + [
            pltpu.VMEM((n2, C * C), F32),
            pltpu.VMEM((n2, C * C), F32),
            pltpu.VMEM((2 * C, C * C), BF16),
            pltpu.VMEM((2 * C, C * C), BF16),
            dma((len(between) + 1,)),
            dma((parts + 6,)),
        ],
        compiler_params=pltpu.CompilerParams(vmem_limit_bytes=VMEM_LIMIT),
    )(*kept, consts["ybt"])
    return (
        grad_field.reshape(rx, ry, depth),
        grad_spectral,
        grad_point,
        grad_bias.reshape(C),
    )


def solution(mesh):
    return jax.shard_map(
        functools.partial(on_device, mesh.shape["gx"], mesh.shape["gy"]),
        mesh=mesh,
        in_specs=(
            P(("groups", "gx"), "gy", None),
            P(("groups", "gx"), "gy", None),
            P(("gx", "gy"), None),
            P(),
            P(),
        ),
        out_specs=(
            P(("groups", "gx"), "gy", None),
            P(("groups", "gx", "gy"), None),
            P("groups", None),
            P("groups"),
        ),
        check_vma=False,
    )
```

```python
import functools
import math

import jax
import jax.numpy as jnp
import numpy as np
from jax import lax
from jax.experimental import pallas as pl
from jax.experimental.pallas import tpu as pltpu
from jax.sharding import PartitionSpec as P

C = 32
KX = 16
KY = 16
KZ = 16
NZ = 32
PM = 2 * KX
F32 = jnp.float32
BF16 = jnp.bfloat16
MESH = pl.DeviceIdType.MESH


def modes(count, length):
    position = np.arange(count)
    return np.where(position < count // 2, position, length - count + position)


def angles(positions, wavenumbers, length):
    steps = positions[:, None] * wavenumbers[None, :] % length
    return 2.0 * math.pi / length * steps.astype(np.float64)


def tables(ngx, ngy, rows_x, rows_y, kk):
    full_x, full_y = ngx * rows_x, ngy * rows_y
    scale = 1.0 / math.sqrt(full_x * full_y * NZ)
    tz = angles(np.arange(NZ), np.arange(KZ), NZ)
    eye = np.eye(C, dtype=np.float32)
    to_modes = np.concatenate(
        [np.kron(f(tz).astype(np.float32), eye) for f in (np.cos, np.sin)], 1
    )
    from_modes = np.concatenate(
        [np.kron(f(tz).astype(np.float32).T, eye) for f in (np.cos, np.sin)], 1
    )
    ty = angles(np.arange(full_y), modes(KY, full_y), full_y).reshape(ngy, rows_y, KY)
    ytab = np.stack([np.cos(ty), -np.sin(ty)], 1).transpose(0, 1, 3, 2)
    ybd = np.einsum("gqjy,xw->gqjxwy", ytab, np.eye(rows_x))
    ybd = ybd.reshape(ngy, 2 * KY * rows_x, rows_x * rows_y)
    tx = angles(np.arange(full_x), modes(KX, full_x), full_x).T
    cx, sx = np.cos(tx) * scale, np.sin(tx) * scale
    xf = np.concatenate(
        [np.concatenate([cx, sx], 1), np.concatenate([-sx, cx], 1)], 0
    )
    bf = lambda a: np.ascontiguousarray(a).astype(jnp.bfloat16)

    def three(a):
        high = bf(a)
        low = bf(a - high.astype(np.float64))
        wide = np.concatenate([high, high, low], 1)
        return np.pad(wide, ((0, -len(wide) % 16), (0, to_modes.shape[1] - wide.shape[1])))

    return dict(
        ybd=jnp.asarray(bf(ybd)),
        gz=jnp.asarray(np.concatenate([bf(to_modes), three(xf), three(xf.T)], 0)),
        ybt=jnp.asarray(bf(ybd.transpose(0, 2, 1))),
        hz=jnp.asarray(bf(from_modes)),
    )


TABLES = ["ybd", "gz", "hz"]
BY_GY = ("ybd", "ybt")
VMEM_LIMIT = 61 * 1024 * 1024


def dot(a, b):
    return jnp.dot(a, b, preferred_element_type=F32)


def dot3(table, b):
    high, low = split(b)
    return dot(table, jnp.concatenate([high, low, high], axis=0))


def split(a):
    high = a.astype(BF16)
    return high, (a - high.astype(F32)).astype(BF16)


def iota(shape, dim):
    return lax.broadcasted_iota(jnp.int32, shape, dim)


def fill(ref, make):
    one = make(iota(ref.shape, 0), iota(ref.shape, 1))
    ref[...] = jnp.where(one, 1.0, 0.0).astype(BF16)


def over_out(r, c):
    return (r & 31) == (c >> 5)


def over_in(r, c):
    return (r & 31) == (c & 31)


def kernel(ngx, ngy, rx, ry, kk, parts, names, *refs):
    it = iter(refs)
    hbm = {name: next(it) for name in names}
    gs_out, gq_out, adj_out, kw_out, tot_out = (next(it) for _ in range(5))
    vm = {name: next(it) for name in names}
    (ybuf, zout, recv1, send2, recv2, zs, recvs, fs, fin, gq, vexp, hexp, red, prod,
     adj, vrow, hrow, acc, accb, kw, pbuf, precv, pbuf2, precv2, f2, pre, gacc, tot, wf, gs,
     perm, permt, ei, eo, ro, ri) = (next(it) for _ in range(36))
    (in_sem, out_sem, s1_send, s1_recv, s2_send, s2_recv, g_send, g_recv, f_send, f_recv,
     p_send, p_recv) = (next(it) for _ in range(12))

    gx, gy = lax.axis_index("gx"), lax.axis_index("gy")
    nx = ngx * rx
    kc = kk // parts
    half = kc * C
    width = 2 * half
    blocks = KZ // kc
    shares = KZ // kk
    n = KX * kc
    modes_in = KZ * C
    xf0, xs0 = NZ * C, NZ * C + PM
    scale = 1.0 / math.sqrt(nx * ngy * ry * NZ)

    loads = {}
    for i, name in enumerate(names):
        src = hbm[name].at[gy] if name in BY_GY else hbm[name]
        loads[name] = pltpu.make_async_copy(src, vm[name], in_sem.at[i])
    early = ("field", "ybd", "gz")
    for name in early:
        loads[name].start()

    barrier = pltpu.get_barrier_semaphore()
    for e in range(1, ngx):
        pl.semaphore_signal(barrier, inc=1, device_id={"gx": lax.rem(gx + e, ngx)}, device_id_type=MESH)
    for d in range(1, ngy):
        pl.semaphore_signal(barrier, inc=1, device_id={"gy": lax.rem(gy + d, ngy)}, device_id_type=MESH)

    def slab(ref, owner, h):
        rows = pl.ds(pl.multiple_of(owner // shares * rx, rx), rx)
        if shares == 1:
            return ref.at[rows, pl.ds(h * width, width)]
        block = owner % shares * parts + h
        return ref.at[rows, pl.ds(pl.multiple_of(block * width, width), width)]

    chips = ngx // 2
    chip, core = gx // 2, gx % 2
    steps = [(c, k) for c in range(1, chips) for k in range(2)] + [(0, 1)]
    peers = [lax.rem(chip + c, chips) * 2 + lax.rem(core + k, 2) for c, k in steps]
    way = 1 - 2 * (gy // (ngy // 2))

    def along(d):
        return lax.rem(gy + way * d + ngy, ngy)

    far_first = list(range(ngy - 1, -1, -1))
    pending = []

    rows = KY * rx

    def forward(t):
        for b in range(2):
            cos = dot(ybuf[...], vm["gz"][: NZ * C, b * 256 : b * 256 + 256])
            sin = dot(ybuf[...], vm["gz"][: NZ * C, modes_in + b * 256 : modes_in + b * 256 + 256])
            real = cos[:rows] + sin[rows:]
            imag = cos[rows:] - sin[:rows]
            part = min(half, 256)
            for i in range(256 // part):
                lane0 = b * 256 + i * part
                at = lane0 // half * width + lane0 % half
                zout[t, :, at : at + part] = real[:, i * part : (i + 1) * part]
                zout[t, :, at + half : at + half + part] = imag[:, i * part : (i + 1) * part]
            if t == 0 and b == 0:
                pl.semaphore_wait(barrier, ngx + ngy - 2)
            if parts == 2:
                send_cells(t, b)
        if parts == 1:
            send_cells(t, 0)

    mine = pl.ds(pl.multiple_of(gx * rx, rx), rx)

    def send_cells(t, h):
        for d in far_first:
            g = along(d)
            for e, to in enumerate(peers):
                copy = pltpu.make_async_remote_copy(
                    src_ref=slab(zout.at[t], to * ngy + g, h),
                    dst_ref=recv1.at[t, h, g, mine],
                    send_sem=s1_send.at[t, h, d, e],
                    recv_sem=s1_recv.at[t, h, g],
                    device_id={"gx": to},
                    device_id_type=MESH,
                )
                copy.start()
                pending.append(copy)
            recv1[t, h, g, mine] = slab(zout.at[t], gx * ngy + g, h)[...]

    def send_sums(t, h):
        for d in far_first:
            g = along(d)
            got = recv1.at[t, h, g, pl.ds(0, (ngx - 1) * rx)]
            pltpu.make_async_copy(got, got, s1_recv.at[t, h, g]).wait()
            both = jnp.concatenate([recv1[t, h, g, :, :half], recv1[t, h, g, :, half:]], axis=0)
            value = dot3(vm["gz"][xf0 : xf0 + PM, : 6 * nx], both)
            if d == 0:
                recv2[t, h, gy] = value
            else:
                send2[t, h, d] = value
                copy = pltpu.make_async_remote_copy(
                    src_ref=send2.at[t, h, d],
                    dst_ref=recv2.at[t, h, gy],
                    send_sem=s2_send.at[t, h, d],
                    recv_sem=s2_recv.at[t, h],
                    device_id={"gy": g},
                    device_id_type=MESH,
                )
                copy.start()
                pending.append(copy)

    def add_sums(t, h):
        got = recv2.at[t, h, pl.ds(0, ngy - 1)]
        pltpu.make_async_copy(got, got, s2_recv.at[t, h]).wait()
        total = recv2[t, h, 0]
        for g in range(1, ngy):
            total = total + recv2[t, h, g]
        return total

    def send_modes(t, h, value):
        zs[t, h] = value
        for d in range(ngy - 1, 0, -1):
            copy = pltpu.make_async_remote_copy(
                src_ref=zs.at[t, h],
                dst_ref=recvs.at[t, h, gy],
                send_sem=g_send.at[t, h, d],
                recv_sem=g_recv.at[t, h, gy],
                device_id={"gy": along(d)},
                device_id_type=MESH,
            )
            copy.start()
            pending.append(copy)
        return_cells(t, h, 0, value)

    def return_cells(t, h, d, block):
        g = along(d)
        if d:
            got = recvs.at[t, h, g]
            pltpu.make_async_copy(got, got, g_recv.at[t, h, g]).wait()
            block = recvs[t, h, g]
        both = dot3(vm["gz"][xs0 : xs0 + 2 * nx, : 3 * PM], block)
        fs[t, h, g, :, :half] = both[:nx]
        fs[t, h, g, :, half:] = both[nx:]
        owner = gx * ngy + g
        for e, to in enumerate(peers):
            copy = pltpu.make_async_remote_copy(
                src_ref=fs.at[t, h, g, pl.ds(pl.multiple_of(to * rx, rx), rx)],
                dst_ref=slab(fin.at[t], owner, h),
                send_sem=f_send.at[t, h, d, e],
                recv_sem=f_recv.at[t, h],
                device_id={"gx": to},
                device_id_type=MESH,
            )
            copy.start()
            pending.append(copy)
        slab(fin.at[t], owner, h)[...] = fs[t, h, g, mine]

    def exchange(t, mix, beside):
        for h in range(parts):
            send_sums(t, h)
            if h == 0:
                beside()
        for h in range(parts):
            send_modes(t, h, mix(h, add_sums(t, h)))
        for h in range(parts):
            for d in range(1, ngy):
                return_cells(t, h, d, None)

    def backward(t, use):
        per = modes_in // parts
        for h in range(parts):
            got = fin.at[t, pl.ds(0, rows // ngx * (ngx - 1)), pl.ds(h * 2 * per, 2 * per)]
            pltpu.make_async_copy(got, got, f_recv.at[t, h]).wait()
            for kb in range(h * blocks // parts, (h + 1) * blocks // parts):
                at, to = kb * width, slice(kb * half, (kb + 1) * half)
                f2[:rows, to] = fin[t, :, at : at + half].astype(BF16)
                f2[rows:, to] = fin[t, :, at + half : at + width].astype(BF16)
            k = slice(h * per, (h + 1) * per)
            for b in range(4):
                at = slice(b * 256, b * 256 + 256)
                cos = dot(f2[:, k], vm["hz"][k, at])
                sin = dot(f2[:, k], vm["hz"][k, NZ * C + b * 256 : NZ * C + b * 256 + 256])
                real, imag = cos[:rows] - sin[rows:], sin[:rows] + cos[rows:]
                if h:
                    real, imag = real + gacc[:rows, at], imag + gacc[rows:, at]
                if h == parts - 1:
                    gq[:rows, at] = real.astype(BF16)
                    gq[rows:, at] = imag.astype(BF16)
                    use(at)
                else:
                    gacc[:rows, at] = real
                    gacc[rows:, at] = imag

    def to_rows(value):
        stack = jnp.concatenate([value[:, k * C : (k + 1) * C] for k in range(kc)], axis=0)
        high = stack.astype(BF16).astype(F32)
        both = jnp.concatenate([high, stack - high], axis=1).astype(BF16)
        return dot(perm[...], both).astype(BF16)

    def from_rows(value):
        high = value.astype(BF16).astype(F32)
        both = jnp.concatenate([high, value - high], axis=1).astype(BF16)
        moved = dot(permt[...], both)
        moved = moved[:, :C] + moved[:, C:]
        return jnp.concatenate([moved[k * PM : (k + 1) * PM] for k in range(kc)], axis=1)

    lane = iota((PM, half), 1)
    first_k = (gx * ngy + gy) % shares * kk

    def doubling(h):
        return jnp.where((lane >> 5) + first_k + h * kc == 0, 1.0, 2.0).astype(F32)

    loads["field"].wait()
    loads["ybd"].wait()
    for b in range(4):
        at = slice(b * 256, b * 256 + 256)
        ybuf[:, at] = dot(vm["ybd"][...], vm["field"][:, at]).astype(BF16)
    loads["gz"].wait()
    for name in names:
        if name not in early:
            loads[name].start()
    forward(0)
    for name in names:
        if name not in early:
            loads[name].wait()

    bits = kc.bit_length() - 1
    fill(perm, lambda r, c: c == (r & (kc - 1)) * PM + (r >> bits))
    fill(permt, lambda r, c: r == (c & (kc - 1)) * PM + (c >> bits))
    fill(ei, over_out)
    fill(eo, over_in)
    fill(ro, lambda r, c: (r & 31) == c)
    fill(ri, lambda r, c: (r >> 5) == c)

    row = iota((256, C), 0) & 31
    col = iota((256, C), 1)
    sel = (row == col).astype(F32).astype(BF16)
    tall = dot(sel, vm["wp"][...]).astype(BF16)
    wide = lax.dot_general(tall, sel, (((1,), (1,)), ((), ())), preferred_element_type=F32)
    br = iota((256, 256), 0) >> 5
    bc = iota((256, 256), 1) >> 5
    kw[...] = jnp.where(br == bc, wide, 0.0).astype(BF16)
    bias = jnp.concatenate([vm["bias"][...]] * 8, axis=1)

    def weights(h, m):
        k = slice(h * kc, (h + 1) * kc)
        return wf[k, m * 2048 : m * 2048 + 1024], wf[k, m * 2048 + 1024 : m * 2048 + 2048]

    def pair(m):
        return slice(m * kc, (m + 1) * kc), slice(n + m * kc, n + (m + 1) * kc)

    def mix_out(h, spec):
        vrow[h] = to_rows(spec)
        vexp[...] = dot(vrow[h], ei[...])
        for m in range(KX):
            a, b = pair(m)
            vr, vi = vexp[a], vexp[b]
            wr, wi = weights(h, m)
            pr = vr * wr - vi * wi
            pi = vr * wi + vi * wr
            red[a] = sum(pr[:, s * 128 : (s + 1) * 128] for s in range(8))
            red[b] = sum(pi[:, s * 128 : (s + 1) * 128] for s in range(8))
        high, low = split(red[...])
        out = dot(high, ro[...]) + dot(low, ro[...])
        return from_rows(out) * doubling(h)

    def mix_in(h, spec):
        hrow[h] = to_rows(spec * doubling(h))
        hexp[...] = dot(hrow[h], eo[...])
        for m in range(KX):
            a, b = pair(m)
            hr, hi = hexp[a], hexp[b]
            wr, wi = weights(h, m)
            prod[a] = hr * wr + hi * wi
            prod[b] = hi * wr - hr * wi
        high, low = split(prod[...])
        out = dot(high, ri[...]) + dot(low, ri[...])
        return from_rows(out)

    def widen():
        for i in range(2 * KX):
            at = slice(i * C * C, (i + 1) * C * C)
            wf[:, at] = vm["weight"][:, at].astype(F32)

    results = []

    def give(src, dst):
        results.append(pltpu.make_async_copy(src, dst, out_sem.at[len(results)]))
        results[-1].start()

    give(kw, kw_out)
    exchange(0, mix_out, widen)

    def cell_work(at):
        v = dot(vm["ybt"][...], gq[:, at]) + pre[:, at]
        root = math.sqrt(2.0 / math.pi)
        square = v * v
        th = jnp.tanh(v * (root + (0.044715 * root) * square))
        slope = 0.5 * (1.0 + th) + v * (1.0 - th * th) * (
            0.5 * root + (1.5 * 0.044715 * root) * square
        )
        value = (vm["cot"][:, at].astype(F32) * slope).astype(BF16)
        adj[:, at] = value
        ybuf[:, at] = dot(vm["ybd"][...], value).astype(BF16)

    for b in range(4):
        at = slice(b * 256, b * 256 + 256)
        pre[:, at] = dot(vm["field"][:, at], kw[...]) + bias
    backward(0, cell_work)
    give(adj, adj_out)
    forward(1)

    def point_gradients():
        ones = jnp.ones((16, rx * ry), BF16)

        grad, total = 0.0, 0.0
        for b in range(4):
            at = slice(b * 256, b * 256 + 256)
            block = adj[:, at]
            grad += lax.dot_general(
                vm["field"][:, at], block, (((0,), (0,)), ((), ())), preferred_element_type=F32
            )
            total += dot(ones, block)
        acc[...] = grad
        accb[...] = total

        pbuf[...] = jnp.zeros_like(pbuf)
        pbuf[:C, :C] = sum(acc[i * C : (i + 1) * C, i * C : (i + 1) * C] for i in range(8)) * scale
        pbuf[C:, :C] = sum(accb[:8, i * C : (i + 1) * C] for i in range(8)) * scale
        for e in range(1, ngx):
            copy = pltpu.make_async_remote_copy(
                src_ref=pbuf,
                dst_ref=precv.at[gx],
                send_sem=p_send.at[e],
                recv_sem=p_recv.at[0],
                device_id={"gx": lax.rem(gx + e, ngx)},
                device_id_type=MESH,
            )
            copy.start()
            pending.append(copy)
        precv[gx] = pbuf[...]

    exchange(1, mix_in, point_gradients)

    got = precv.at[pl.ds(0, ngx - 1)]
    pltpu.make_async_copy(got, got, p_recv.at[0]).wait()
    pbuf2[...] = sum(precv[i] for i in range(ngx))
    for d in range(1, ngy):
        copy = pltpu.make_async_remote_copy(
            src_ref=pbuf2,
            dst_ref=precv2.at[gy],
            send_sem=p_send.at[ngx + d],
            recv_sem=p_recv.at[1],
            device_id={"gy": lax.rem(gy + d, ngy)},
            device_id_type=MESH,
        )
        copy.start()
        pending.append(copy)
    precv2[gy] = pbuf2[...]

    for h in range(parts):
        k = slice(h * kc, (h + 1) * kc)
        vexp[...] = dot(vrow[h], ei[...])
        hexp[...] = dot(hrow[h], eo[...])
        for m in range(KX):
            a, b = pair(m)
            vr, vi, hr, hi = vexp[a], vexp[b], hexp[a] * scale, hexp[b] * scale
            gs[k, m * 2048 : m * 2048 + 1024] = vr * hr + vi * hi
            gs[k, m * 2048 + 1024 : m * 2048 + 2048] = vr * hi - vi * hr
    give(gs, gs_out)
    backward(1, lambda at: None)
    give(gq, gq_out)
    got = precv2.at[pl.ds(0, ngy - 1)]
    pltpu.make_async_copy(got, got, p_recv.at[1]).wait()
    tot[...] = sum(precv2[i] for i in range(ngy))
    give(tot, tot_out)
    for copy in results:
        copy.wait()
    for copy in pending:
        copy.wait_send()


def finish(*refs):
    (gs_in, gq_in, adj_in, kw_in, tot_in, ybt_in, gf_out, gs_out, gp_out, gb_out,
     gs, gq, adj, kw, tot, ybt, gf, gp, gb, in_sem, out_sem) = refs
    cuts = 4
    lanes = gs.shape[1] // cuts
    pieces = [pl.ds(i * lanes, lanes) for i in range(cuts)]
    pairs = [(gq_in, gq), (adj_in, adj), (kw_in, kw), (ybt_in.at[lax.axis_index("gy")], ybt),
             (tot_in, tot)]
    pairs += [(gs_in.at[:, at], gs.at[:, at]) for at in pieces]
    loads = [pltpu.make_async_copy(a, b, in_sem.at[i]) for i, (a, b) in enumerate(pairs)]
    for load in loads:
        load.start()
    results = []

    def give(src, dst):
        results.append(pltpu.make_async_copy(src, dst, out_sem.at[len(results)]))
        results[-1].start()

    for load in loads[:4]:
        load.wait()
    for b in range(4):
        at = pl.ds(b * 256, 256)
        back = lax.dot_general(
            adj[:, at], kw[...], (((1,), (1,)), ((), ())), preferred_element_type=F32
        )
        gf[:, at] = (dot(ybt[...], gq[:, at]) + back).astype(BF16)
        give(gf.at[:, at], gf_out.at[:, at])
        loads[5 + b].wait()
        give(gs.at[:, pieces[b]], gs_out.at[:, pieces[b]])
    loads[4].wait()
    gp[...] = tot[:C, :C]
    gb[...] = tot[C : C + 1, :C]
    give(gp, gp_out)
    give(gb, gb_out)
    for copy in results:
        copy.wait()


def on_device(ngx, ngy, field_input, cotangent, spectral_weight, point_weight, point_bias):
    rx, ry, depth = field_input.shape
    kk = spectral_weight.shape[0]
    cells = rx * ry
    nx = rx * ngx
    parts = 2 if kk == KZ else 1
    kc = kk // parts
    half, width = kc * C, 2 * kc * C
    arrays = dict(field=field_input.reshape(cells, depth))
    consts = tables(ngx, ngy, rx, ry, kk)
    arrays["ybd"] = consts["ybd"]
    arrays["gz"] = consts["gz"]
    arrays["weight"] = spectral_weight
    for name in TABLES:
        arrays[name] = consts[name]
    arrays["ybt"] = consts["ybt"]
    arrays["cot"] = cotangent.reshape(cells, depth)
    arrays["wp"] = point_weight
    arrays["bias"] = point_bias.reshape(1, C)
    names = tuple(arrays)
    local = [
        pltpu.VMEM(a.shape[1:] if k in BY_GY else a.shape, a.dtype) for k, a in arrays.items()
    ]
    rows = KY * rx
    n2 = PM * kc
    hbm = pl.BlockSpec(memory_space=pltpu.HBM)
    dma = pltpu.SemaphoreType.DMA
    between = (
        jax.ShapeDtypeStruct(spectral_weight.shape, F32),
        jax.ShapeDtypeStruct((2 * rows, depth), BF16),
        jax.ShapeDtypeStruct((cells, depth), BF16),
        jax.ShapeDtypeStruct((256, 256), BF16),
        jax.ShapeDtypeStruct((C + 8, 128), F32),
    )

    def room(types):
        return [pltpu.VMEM(a.shape, a.dtype) for a in types]

    kept = pl.pallas_call(
        functools.partial(kernel, ngx, ngy, rx, ry, kk, parts, names),
        out_shape=between,
        in_specs=[hbm] * len(names),
        out_specs=(hbm,) * len(between),
        scratch_shapes=local
        + [
            pltpu.VMEM((2 * rows, depth), BF16),
            pltpu.VMEM((2, rows, depth), F32),
            pltpu.VMEM((2, parts, ngy, nx, width), F32),
            pltpu.VMEM((2, parts, ngy, PM, half), F32),
            pltpu.VMEM((2, parts, ngy, PM, half), F32),
            pltpu.VMEM((2, parts, PM, half), F32),
            pltpu.VMEM((2, parts, ngy, PM, half), F32),
            pltpu.VMEM((2, parts, ngy, nx, width), F32),
            pltpu.VMEM((2, rows, depth), F32),
            pltpu.VMEM((2 * rows, depth), BF16),
            pltpu.VMEM((n2, C * C), F32),
            pltpu.VMEM((n2, C * C), F32),
            pltpu.VMEM((n2, 128), F32),
            pltpu.VMEM((n2, C * C), F32),
            pltpu.VMEM((cells, depth), BF16),
            pltpu.VMEM((parts, n2, 2 * C), BF16),
            pltpu.VMEM((parts, n2, 2 * C), BF16),
            pltpu.VMEM((256, 256), F32),
            pltpu.VMEM((16, 256), F32),
            pltpu.VMEM((256, 256), BF16),
            pltpu.VMEM((C + 8, 128), F32),
            pltpu.VMEM((ngx, C + 8, 128), F32),
            pltpu.VMEM((C + 8, 128), F32),
            pltpu.VMEM((ngy, C + 8, 128), F32),
            pltpu.VMEM((2 * rows, KZ * C), BF16),
            pltpu.VMEM((cells, depth), F32),
            pltpu.VMEM((2 * rows, depth), F32),
            pltpu.VMEM((C + 8, 128), F32),
            pltpu.VMEM(spectral_weight.shape, F32),
            pltpu.VMEM(spectral_weight.shape, F32),
            pltpu.VMEM((n2, n2), BF16),
            pltpu.VMEM((n2, n2), BF16),
            pltpu.VMEM((2 * C, C * C), BF16),
            pltpu.VMEM((2 * C, C * C), BF16),
            pltpu.VMEM((128, C), BF16),
            pltpu.VMEM((C * C, C), BF16),
            dma((len(names),)),
            dma((len(between),)),
            dma((2, parts, ngy, ngx - 1)),
            dma((2, parts, ngy)),
            dma((2, parts, ngy)),
            dma((2, parts)),
            dma((2, parts, ngy)),
            dma((2, parts, ngy)),
            dma((2, parts, ngy, ngx - 1)),
            dma((2, parts)),
            dma((ngx + ngy,)),
            dma((2,)),
        ],
        compiler_params=pltpu.CompilerParams(
            collective_id=0, has_side_effects=True, vmem_limit_bytes=VMEM_LIMIT
        ),
    )(*arrays.values())
    wanted = (
        jax.ShapeDtypeStruct((cells, depth), BF16),
        jax.ShapeDtypeStruct(spectral_weight.shape, F32),
        jax.ShapeDtypeStruct((C, C), F32),
        jax.ShapeDtypeStruct((1, C), F32),
    )
    grad_field, grad_spectral, grad_point, grad_bias = pl.pallas_call(
        finish,
        out_shape=wanted,
        in_specs=[hbm] * (len(between) + 1),
        out_specs=(hbm,) * len(wanted),
        scratch_shapes=room(between)
        + [pltpu.VMEM(consts["ybt"].shape[1:], BF16)]
        + room(wanted[:1] + wanted[2:])
        + [dma((len(between) + 5,)), dma((10,))],
        compiler_params=pltpu.CompilerParams(vmem_limit_bytes=VMEM_LIMIT),
    )(*kept, consts["ybt"])
    return (
        grad_field.reshape(rx, ry, depth),
        grad_spectral,
        grad_point,
        grad_bias.reshape(C),
    )


def solution(mesh):
    return jax.shard_map(
        functools.partial(on_device, mesh.shape["gx"], mesh.shape["gy"]),
        mesh=mesh,
        in_specs=(
            P(("groups", "gx"), "gy", None),
            P(("groups", "gx"), "gy", None),
            P(("gx", "gy"), None),
            P(),
            P(),
        ),
        out_specs=(
            P(("groups", "gx"), "gy", None),
            P(("groups", "gx", "gy"), None),
            P("groups", None),
            P("groups"),
        ),
        check_vma=False,
    )
```
